256 devices in a mesh: freq: 8 (over x, y_hi), space: 32 (over z, y_lo, core).
Axes of the slice: x: 4, y: 4 (y_hi: 2, y_lo: 2; y = y_hi * 2 + y_lo), z: 8, core: 2. Of those that a mesh axis runs over, the one named last changes fastest.
Arguments:
- source_current: float32 [8, 2, 2, 3, 128, 16, 256], P('freq', None, None, None, 'space'), may hold values from -60 to 60
- conductivity: float32 [128, 16, 256], P('space', None, 'freq'), may hold values from 1 to 10
- frequency: float32 [8], P('freq'), may hold values from 4 to 16
- station_cells: int32 [2048], P('space'), may hold values from 0 to 1023
- station_depth: int32 [2048], P('space'), may hold values from 0 to 15
Outputs:
- electric_field: float32 [8, 2, 2, 3, 128, 16, 256], P('freq', None, None, None, 'space')
- predicted: float32 [8, 2, 2, 3, 2048], P('freq', None, None, None, 'space')
- gradient: float32 [128, 16, 256], P('space', None, 'freq')
The draws below stay inside these ranges and needn't reach their ends.
Inputs may be any that keep to these rules, and one draw needn't show every extreme that they name: `station_cells`: A station's cell lies in the tile of the devices that hold the station. `station_depth`: depth index of a station's cell.
All inputs are finite; a program needn't handle non-finite values.
Results may differ from the reference program's by a relative error of at most 0.00026.
Values sent between devices are 32-bit elements; how exact they have to be, the bound alone decides.
No kernel may reach another device: no remote copies, remote signals or barrier semaphores. Data moves between devices by JAX's collectives and lax.ppermute only.
A program may use at most 64 MiB of HBM per device.

```python
import math
import jax
import jax.numpy as jnp
from jax import lax

CX = 4
NY = 256
NZ = 16
POLS = 2
ITERS = 2
STA_DEV = 64
FREQS = 8
NX = 128
STATIONS = 2048


def touch_ends(entries, stream_key, least, top_value):
    dims = entries.shape
    place = [jax.random.randint(jax.random.fold_in(stream_key, axis), (), 0, dims[axis]) for axis in range(len(dims))]
    entries = entries.at[tuple(place)].set(least)
    longest = dims.index(max(dims))
    place[longest] = (place[longest] + 1) % dims[longest]
    return entries.at[tuple(place)].set(top_value)


def level_of(stream_key, extent, shards, least, top_value):
    def one(dim, blocks):
        steps = jax.random.uniform(jax.random.fold_in(jax.random.fold_in(stream_key, 6), dim), (blocks,), jnp.float32, least / len(shards), top_value / len(shards))
        return jnp.repeat(jnp.exp(steps), extent[dim] // blocks).reshape((-1,) + (1,) * (len(extent) - dim - 1))

    gain = one(*shards[0])
    for cut in shards[1:]:
        gain = gain * one(*cut)
    return gain


def centred(key, extent, width, most, shards=(), held_as=jnp.bfloat16):
    loudness = level_of(key, extent, shards, -0.22, 0.18) if shards else 1.0
    values = jax.random.normal(key, extent, jnp.float32) * width * loudness
    return jnp.minimum(jnp.maximum(values, -most), most).astype(held_as)


def setup_inputs(seed: int = 0) -> dict:
    splits = jax.random.split(jax.random.key(seed), 6)
    source_current = centred(splits[0], (FREQS, POLS, 2, 3, NX, NZ, NY), 10.0, 60.0, ((0, 8), (4, 32)), jnp.float32)
    conductivity = jnp.clip(jnp.exp(math.log(10.0) - 2.3025851 * jax.random.uniform(splits[1], (NX, NZ, NY), jnp.float32) ** level_of(splits[1], (NX, NZ, NY), ((0, 32), (2, 8)), -0.2, 0.2)), 1.0, 10.0)
    frequency = jnp.clip(jnp.exp(math.log(16.0) - 1.3862944 * jax.random.uniform(splits[2], (FREQS,), jnp.float32) ** level_of(splits[2], (FREQS,), ((0, 8),), -0.2, 0.2)), 4.0, 16.0)
    station_cells = touch_ends(jax.random.randint(splits[3], (STATIONS,), 0, CX * NY), jax.random.fold_in(splits[3], 1), 0, (CX * NY) - 1).astype(jnp.int32)
    station_depth = touch_ends(jax.random.randint(splits[4], (STATIONS,), 0, NZ), jax.random.fold_in(splits[4], 1), 0, NZ - 1).astype(jnp.int32)
    return dict(source_current=source_current, conductivity=conductivity, frequency=frequency, station_cells=station_cells, station_depth=station_depth)


def forward_x(array_in):
    return array_in[..., 1:, :-1, :-1] - array_in[..., :-1, :-1, :-1]


def forward_z(array_in):
    return array_in[..., :, 1:, :-1] - array_in[..., :, :-1, :-1]


def forward_y(array_in):
    return array_in[..., :, :-1, 1:] - array_in[..., :, :-1, :-1]


def backward_x(array_in):
    return array_in[..., 1:, 1:, 1:] - array_in[..., :-1, 1:, 1:]


def backward_z(array_in):
    return array_in[..., :, 1:, 1:] - array_in[..., :, :-1, 1:]


def backward_y(array_in):
    return array_in[..., :, 1:, 1:] - array_in[..., :, 1:, :-1]


def magnetic(edge_x, edge_y, edge_z):
    inner_y = edge_y[..., :-1, :, :]
    inner_z = edge_z[..., :-1, :, :]
    face_x = forward_y(inner_z) - forward_z(inner_y)
    face_y = forward_z(edge_x) - forward_x(edge_z)
    face_z = forward_x(edge_y) - forward_y(edge_x)
    return face_x, face_y, face_z


def curl_back(face_x, face_y, face_z):
    trim_y = face_y[..., 1:, :, :]
    trim_z = face_z[..., 1:, :, :]
    curl_x = backward_y(trim_z) - backward_z(trim_y)
    curl_y = backward_z(face_x) - backward_x(face_z)
    curl_z = backward_x(face_y) - backward_y(face_x)
    return jnp.stack([curl_x, curl_y, curl_z], axis=-4)


def curl_padded(padded):
    faces = magnetic(padded[..., 0, :-1, :, :], padded[..., 1, :, :, :], padded[..., 2, :, :, :])
    return curl_back(faces[0][..., 1:, :, :], faces[1], faces[2])


def operate(electric, damping, orient):
    pad_width = [(0, 0)] * (electric.ndim - 3) + [(1, 1)] * 3
    curl = curl_padded(jnp.pad(electric, pad_width))
    real = curl[..., 0, :, :, :, :] - orient * damping * electric[..., 1, :, :, :, :]
    imag = curl[..., 1, :, :, :, :] + orient * damping * electric[..., 0, :, :, :, :]
    return jnp.stack([real, imag], axis=-5)


def inner_product(left, right):
    real = jnp.sum(left[:, 0] * right[:, 0] + left[:, 1] * right[:, 1], axis=(1, 2, 3, 4))
    imag = jnp.sum(left[:, 0] * right[:, 1] - left[:, 1] * right[:, 0], axis=(1, 2, 3, 4))
    return jnp.stack([real, imag])


def times_complex(left, right):
    return jnp.stack([left[0] * right[0] - left[1] * right[1], left[0] * right[1] + left[1] * right[0]])


def divide_complex(left, right):
    denom = right[0] * right[0] + right[1] * right[1]
    return jnp.stack([(left[0] * right[0] + left[1] * right[1]) / denom, (left[1] * right[0] - left[0] * right[1]) / denom])


def conjugate(value):
    return jnp.stack([value[0], -value[1]])


def scale_field(factor, electric):
    real_part = factor[0][:, None, None, None, None]
    imag_part = factor[1][:, None, None, None, None]
    return jnp.stack([real_part * electric[:, 0] - imag_part * electric[:, 1], real_part * electric[:, 1] + imag_part * electric[:, 0]], axis=1)


def solve(rhs, damping):
    solution = jnp.zeros_like(rhs)
    adjoint = jnp.zeros_like(rhs)
    residual = rhs
    shadow_res = rhs
    direction = rhs
    shadow_dir = rhs
    rho_now = inner_product(shadow_res, residual)
    for step in range(ITERS):
        image = operate(direction, damping, 1.0)
        shadow_img = operate(shadow_dir, damping, -1.0)
        step_size = divide_complex(rho_now, inner_product(shadow_dir, image))
        solution = solution + scale_field(step_size, direction)
        residual = residual - scale_field(step_size, image)
        adjoint = adjoint + scale_field(conjugate(step_size), shadow_dir)
        shadow_res = shadow_res - scale_field(conjugate(step_size), shadow_img)
        if step + 1 < ITERS:
            rho_next = inner_product(shadow_res, residual)
            ratio_next = divide_complex(rho_next, rho_now)
            direction = residual + scale_field(ratio_next, direction)
            shadow_dir = shadow_res + scale_field(conjugate(ratio_next), shadow_dir)
            rho_now = rho_next
    return solution, adjoint


def reference(source_current, conductivity, frequency, station_cells, station_depth):
    station_ids = jnp.arange(STATIONS, dtype=jnp.int32)
    global_x = (station_ids // STA_DEV) * CX + station_cells // NY
    flat_index = ((global_x * NZ + station_depth) * NY + station_cells % NY).astype(jnp.int32)

    def one_frequency(inputs):
        rhs, omega_value = inputs
        damping = omega_value * conductivity
        solution, adjoint = solve(rhs, damping)
        sampled = jnp.take(solution.reshape(POLS * 6, -1), flat_index, axis=1).reshape(POLS, 2, 3, STATIONS)
        sensitivity = omega_value * jnp.sum(adjoint[:, 0] * solution[:, 0] - adjoint[:, 1] * solution[:, 1], axis=(0, 1))
        return solution, sampled, sensitivity

    electric_field, predicted, terms = lax.map(one_frequency, (source_current, frequency))
    gradient = conductivity * jnp.sum(terms, axis=0) / (3.0 * POLS * FREQS)
    return electric_field, predicted, gradient
```

```python
import functools
import jax
import jax.numpy as jnp
from jax import lax
from jax.experimental import pallas as pl
from jax.experimental.pallas import tpu as pltpu
from jax.sharding import PartitionSpec as P

F32 = jnp.float32
N_FREQ = 8
N_SPACE = 32
DEPTH = 16
WIDTH = 256
PLANES = 4
SLAB = WIDTH // N_FREQ
LIMIT = 24 * 1024 * 1024


def params():
    return pltpu.CompilerParams(vmem_limit_bytes=LIMIT)


def vmem():
    return pl.BlockSpec(memory_space=pltpu.VMEM)


def anywhere():
    return pl.BlockSpec(memory_space=pl.ANY)


def smem():
    return pl.BlockSpec(memory_space=pltpu.SMEM)


def iota(dim, shape=(DEPTH, WIDTH)):
    return lax.broadcasted_iota(jnp.int32, shape, dim)


class Stencil:
    def __init__(self):
        row, lane = iota(0), iota(1)
        self.first_row, self.last_row = row == 0, row == DEPTH - 1
        self.first_lane, self.last_lane = lane == 0, lane == WIDTH - 1

    def fy(self, f):
        return jnp.where(self.last_lane, 0.0, pltpu.roll(f, WIDTH - 1, 1)) - f

    def fz(self, f):
        return jnp.where(self.last_row, 0.0, pltpu.roll(f, DEPTH - 1, 0)) - f

    def by(self, g, before):
        return g - jnp.where(self.first_lane, before, pltpu.roll(g, 1, 1))

    def bz(self, g, before):
        return g - jnp.where(self.first_row, before, pltpu.roll(g, 1, 0))

    def faces_yz(self, ex, ey, ez, ey_next, ez_next):
        return self.fz(ex) - (ez_next - ez), (ey_next - ey) - self.fy(ex)

    def face_x(self, ey, ez):
        return self.fy(ez) - self.fz(ey)

    def edge_terms(self, px, py, pz):
        return jnp.where(self.first_lane, px + pz, 0.0) + jnp.where(self.first_row, px + py, 0.0)


def fold(plane):
    half = plane[:8] + plane[8:]
    return half[:, :128] + half[:, 128:]


def dot3(a, b):
    return a[0] * b[0] + a[1] * b[1] + a[2] * b[2]


def send_kernel(b_ref, right_ref, left_ref, sems):
    copies = [
        pltpu.make_async_copy(b_ref.at[:, :, :, 0], right_ref.at[:, :, pl.ds(0, 3)], sems.at[0]),
        pltpu.make_async_copy(b_ref.at[:, :, pl.ds(1, 2), 1], right_ref.at[:, :, pl.ds(3, 2)], sems.at[1]),
        pltpu.make_async_copy(b_ref.at[:, :, :, PLANES - 1], left_ref, sems.at[2]),
    ]
    for copy in copies:
        copy.start()
    for copy in copies:
        copy.wait()


def pack_kernel(own_ref, next_ref, out_ref):
    own = jnp.concatenate([own_ref[i] for i in range(PLANES)], axis=1)
    after = jnp.concatenate([next_ref[0]] * PLANES, axis=1)
    for f in range(N_FREQ):
        out_ref[f, 0] = own
        out_ref[f, 1] = after


def curl_kernel(b_ref, low_ref, high_ref, u_ref, unext_ref, face_ref, t_ref, acc_ref):
    st = Stencil()
    place = lax.axis_index("space")
    keep_next = jnp.where(place == N_SPACE - 1, 0.0, 1.0).astype(F32)
    is_first = jnp.where(place == 0, 1.0, 0.0).astype(F32)

    def one_pol(pol, carry):
        s0 = jnp.zeros((8, 128), F32)
        s1 = jnp.zeros((8, 128), F32)
        s2 = jnp.zeros((8, 128), F32)
        s3 = jnp.zeros((8, 128), F32)
        for part in range(2):
            def field(c, i):
                if i < 0:
                    return low_ref[pol, part, c]
                if i < PLANES:
                    return b_ref[pol, part, c, i]
                if i == PLANES:
                    return high_ref[pol, part, c]
                return high_ref[pol, part, c + 2]

            hy_old, hz_old = st.faces_yz(field(0, -1), field(1, -1), field(2, -1), field(1, 0), field(2, 0))
            u_old = None
            for i in range(PLANES + 1):
                ex, ey, ez = field(0, i), field(1, i), field(2, i)
                hx = st.face_x(ey, ez)
                hy, hz = st.faces_yz(ex, ey, ez, field(1, i + 1), field(2, i + 1))
                uy = st.bz(hx, -ey) - (hz - hz_old)
                uz = (hy - hy_old) - st.by(hx, ez)
                hy_old, hz_old = hy, hz
                if i < PLANES:
                    ux = st.by(hz, -ex) - st.bz(hy, ex)
                    u_ref[pol, part, 0, i] = ux
                    u_ref[pol, part, 1, i] = uy
                    u_ref[pol, part, 2, i] = uz
                    s0 = s0 + fold(ex * ex + ey * ey + ez * ez)
                    s1 = s1 + fold(ex * ux + ey * uy + ez * uz)
                else:
                    uy = uy * keep_next
                    uz = uz * keep_next
                    unext_ref[pol, part, 0] = uy
                    unext_ref[pol, part, 1] = uz
                if u_old is not None:
                    px, py, pz = u_old
                    fx = st.face_x(py, pz)
                    fy, fz = st.faces_yz(px, py, pz, uy, uz)
                    face_ref[pol, part, 0, i - 1] = fx
                    face_ref[pol, part, 1, i - 1] = fy
                    face_ref[pol, part, 2, i - 1] = fz
                    qx, qy, qz = px * px, py * py, pz * pz
                    s2 = s2 + fold(qx + qy + qz)
                    total = fx * fx + fy * fy + fz * fz + st.edge_terms(qx, qy, qz)
                    if i == 1:
                        total = total + is_first * (qy + qz)
                    s3 = s3 + fold(total)
                if i < PLANES:
                    u_old = (ux, uy, uz)
        acc_ref[pol, 0] = s0
        acc_ref[pol, 1] = s1
        acc_ref[pol, 2] = s2
        acc_ref[pol, 3] = s3
        for i in range(PLANES):
            br = [b_ref[pol, 0, c, i] for c in range(3)]
            bi = [b_ref[pol, 1, c, i] for c in range(3)]
            ur = [u_ref[pol, 0, c, i] for c in range(3)]
            ui = [u_ref[pol, 1, c, i] for c in range(3)]
            t_ref[pol, 0, i] = dot3(br, br) - dot3(bi, bi)
            t_ref[pol, 1, i] = dot3(ur, ur) - dot3(ui, ui)
            t_ref[pol, 2, i] = dot3(br, ur) - dot3(bi, ui)
        return carry

    lax.fori_loop(0, 2, one_pol, 0)


N_SUMS = 12


def moment_kernel(got_ref, b_ref, high_ref, u_ref, face_ref, acc_ref, sigma_ref, sums_ref, next_ref):
    st = Stencil()
    is_first = jnp.where(lax.axis_index("space") == 0, 1.0, 0.0).astype(F32)
    group = iota(1, (DEPTH, 128)) // SLAB
    for half in range(2):
        cols = pl.ds(128 * half, 128)
        for i in range(PLANES + 1):
            value = None
            for q in range(4):
                piece = got_ref[4 * half + q, 0 if i < PLANES else 1]
                shift = (SLAB * (q - i)) % 128 if i < PLANES else 0
                piece = pltpu.roll(piece, shift, 1) if shift else piece
                value = piece if value is None else jnp.where(group == q, piece, value)
            if i < PLANES:
                sigma_ref[i, :, cols] = value
            else:
                next_ref[:, cols] = value

    lane = iota(1, (1, 128))

    def one_pol(pol, row):
        names = ("d1", "d2", "d3", "e1", "e2", "g", "x1", "x2")
        acc = {name: jnp.zeros((8, 128), F32) for name in names}

        def add(name, plane):
            acc[name] = acc[name] + fold(plane)

        for part in range(2):
            after = next_ref[...]
            wy_next = after * high_ref[pol, part, 1]
            wz_next = after * high_ref[pol, part, 2]
            for i in reversed(range(PLANES)):
                s = sigma_ref[i]
                b = [b_ref[pol, part, c, i] for c in range(3)]
                u = [u_ref[pol, part, c, i] for c in range(3)]
                w = [s * f for f in b]
                fx = st.face_x(w[1], w[2])
                fy, fz = st.faces_yz(w[0], w[1], w[2], wy_next, wz_next)
                wy_next, wz_next = w[1], w[2]
                gx, gy, gz = [face_ref[pol, part, c, i] for c in range(3)]
                rx, ry, rz = [f * f for f in w]
                qx, qy, qz = [f * v for f, v in zip(w, u)]
                ww = rx + ry + rz
                uw = qx + qy + qz
                x1 = fx * gx + fy * gy + fz * gz + st.edge_terms(qx, qy, qz)
                x2 = fx * fx + fy * fy + fz * fz + st.edge_terms(rx, ry, rz)
                if i == 0:
                    x1 = x1 + is_first * (qy + qz)
                    x2 = x2 + is_first * (ry + rz)
                add("x1", x1)
                add("x2", x2)
                add("d1", dot3(w, b))
                add("d2", ww)
                add("d3", s * ww)
                add("e1", uw)
                add("e2", s * dot3(u, u))
                add("g", s * uw)
        every = [acc_ref[pol, k] for k in range(4)] + [acc[name] for name in names]
        for k, value in enumerate(every):
            row = row + jnp.where(lane == k + 64 * pol, jnp.sum(value, axis=(0, 1), keepdims=True), 0.0)
        return row

    row = lax.fori_loop(0, 2, one_pol, jnp.zeros((1, 128), F32))
    for k in range(N_SPACE):
        sums_ref[k] = row


def times(a, b):
    return a[0] * b[0] - a[1] * b[1], a[0] * b[1] + a[1] * b[0]


def over(a, b):
    denom = b[0] * b[0] + b[1] * b[1]
    return (a[0] * b[0] + a[1] * b[1]) / denom, (a[1] * b[0] - a[0] * b[1]) / denom


def steps(sums_ref, omega):
    row = jnp.sum(jnp.concatenate([sums_ref[k] for k in range(N_SPACE)], axis=0), axis=0, keepdims=True)
    found = []
    for pol in range(2):
        s0, s1, s2, s3, d1, d2, d3, e1, e2, g, x1, x2 = [
            row[:, k + 64 * pol : k + 64 * pol + 1] for k in range(N_SUMS)
        ]
        w2 = omega * omega
        m0 = (s0, jnp.zeros_like(s0))
        m1 = (s1, omega * d1)
        m2 = (s2 - w2 * d2, 2.0 * omega * e1)
        m3 = (s3 - w2 * (2.0 * g + x2), omega * (2.0 * x1 + e2) - omega * w2 * d3)
        a0 = over(m0, m1)
        a0a0 = times(a0, a0)
        z = times(a0a0, m2)
        rho = (z[0] - s0, z[1])
        grow = (1.0 + rho[0] / s0, rho[1] / s0)
        first = times(times(grow, grow), m1)
        second = times(times(a0, grow), m2)
        third = times(a0a0, m3)
        curv = (first[0] - 2.0 * second[0] + third[0], first[1] - 2.0 * second[1] + third[1])
        a1 = over(rho, curv)
        a1g = times(a1, grow)
        a1a0 = times(a1, a0)
        found.append(((a0[0] + a1g[0], a0[1] + a1g[1]), (-a1a0[0], -a1a0[1])))
    return found


def sense_kernel(omega_ref, sums_ref, t_ref, sigma_ref, out_ref):
    omega = omega_ref[0]
    found = steps(sums_ref, omega)
    group = iota(1, (DEPTH, 128)) // SLAB
    planes = []
    for i in range(PLANES):
        scaled = omega * sigma_ref[i]
        total = jnp.zeros((DEPTH, WIDTH), F32)
        for pol in range(2):
            c0, c1 = found[pol]
            fr = c0[0] - scaled * c1[1]
            fi = c0[1] + scaled * c1[0]
            total = total + (fr * fr + fi * fi) * t_ref[pol, 0, i]
            total = total + (c1[0] * c1[0] + c1[1] * c1[1]) * t_ref[pol, 1, i]
            total = total + 2.0 * (fr * c1[0] + fi * c1[1]) * t_ref[pol, 2, i]
        planes.append(omega * total)
    for f in range(N_FREQ):
        half, q = f // 4, f % 4
        value = None
        for i in range(PLANES):
            piece = planes[i][:, 128 * half : 128 * half + 128]
            shift = (SLAB * (i - q)) % 128
            piece = pltpu.roll(piece, shift, 1) if shift else piece
            value = piece if value is None else jnp.where(group == i, piece, value)
        out_ref[f] = value


def field_kernel(omega_ref, sums_ref, b_ref, u_ref, sigma_ref, cells_ref, depth_ref, x_ref, sampled_ref):
    omega = omega_ref[0]
    found = steps(sums_ref, omega)
    cells, depth = cells_ref[...], depth_ref[...]
    stations = cells.shape[1]
    in_row = iota(0, (PLANES * DEPTH, stations)) == cells // WIDTH * DEPTH + depth
    in_lane = (iota(0, (WIDTH, stations)) == cells % WIDTH).astype(F32)
    for pol in range(2):
        c0, c1 = found[pol]
        for i in range(PLANES):
            scaled = omega * sigma_ref[i]
            fr = c0[0] - scaled * c1[1]
            fi = c0[1] + scaled * c1[0]
            for c in range(3):
                br, bi = b_ref[pol, 0, c, i], b_ref[pol, 1, c, i]
                ur, ui = u_ref[pol, 0, c, i], u_ref[pol, 1, c, i]
                x_ref[pol, 0, c, i] = fr * br - fi * bi + c1[0] * ur - c1[1] * ui
                x_ref[pol, 1, c, i] = fr * bi + fi * br + c1[0] * ui + c1[1] * ur
        for part in range(2):
            for c in range(3):
                rows = x_ref[pol, part, c].reshape(PLANES * DEPTH, WIDTH)
                picked = jnp.dot(rows, in_lane, precision=lax.Precision.HIGHEST, preferred_element_type=F32)
                sampled_ref[pol, part, pl.ds(c, 1)] = jnp.sum(
                    jnp.where(in_row, picked, 0.0), axis=0, keepdims=True
                )


def gradient_kernel(terms_ref, own_ref, out_ref):
    total = terms_ref[0]
    for f in range(1, N_FREQ):
        total = total + terms_ref[f]
    for i in range(PLANES):
        out_ref[i] = own_ref[i] * total[:, SLAB * i : SLAB * i + SLAB] * (1.0 / (3.0 * 2 * N_FREQ))


def shape(*dims):
    return jax.ShapeDtypeStruct(dims, F32)


def cost(us):
    return pl.CostEstimate(flops=0, bytes_accessed=int(us * 3.0e6), transcendentals=0)


def local(source_current, conductivity, frequency, station_cells, station_depth):
    b = source_current[0]
    stations = station_cells.shape[0]
    ends = N_SPACE - 1
    upward = [(i, i + 1) for i in range(ends)]
    downward = [(i + 1, i) for i in range(ends)]

    next_sigma = lax.ppermute(conductivity[:1], "space", downward)
    to_left, to_right = pl.pallas_call(
        send_kernel,
        out_shape=(shape(2, 2, 5, DEPTH, WIDTH), shape(2, 2, 3, DEPTH, WIDTH)),
        in_specs=[anywhere()],
        out_specs=(anywhere(), anywhere()),
        scratch_shapes=[pltpu.SemaphoreType.DMA((3,))],
        compiler_params=params(),
        name="halo_planes",
    )(b)
    high = lax.ppermute(to_left, "space", downward)
    low = lax.ppermute(to_right, "space", upward)
    packed = pl.pallas_call(
        pack_kernel,
        out_shape=shape(N_FREQ, 2, DEPTH, 128),
        in_specs=[vmem(), vmem()],
        out_specs=vmem(),
        compiler_params=params(),
        name="pack_conductivity",
    )(conductivity, next_sigma)
    got = lax.all_to_all(packed, "freq", 0, 0)

    u, _, faces, products, acc = pl.pallas_call(
        curl_kernel,
        out_shape=(
            shape(2, 2, 3, PLANES, DEPTH, WIDTH),
            shape(2, 2, 2, DEPTH, WIDTH),
            shape(2, 2, 3, PLANES, DEPTH, WIDTH),
            shape(2, 3, PLANES, DEPTH, WIDTH),
            shape(2, 4, 8, 128),
        ),
        in_specs=[vmem()] * 3,
        out_specs=(vmem(),) * 5,
        compiler_params=params(),
        cost_estimate=cost(3.0),
        name="curl_curl",
    )(b, low, high)
    sigma, sums = pl.pallas_call(
        moment_kernel,
        out_shape=(shape(PLANES, DEPTH, WIDTH), shape(N_SPACE, 1, 128)),
        in_specs=[vmem()] * 6,
        out_specs=(vmem(),) * 2,
        scratch_shapes=[pltpu.VMEM((DEPTH, WIDTH), F32)],
        compiler_params=params(),
        cost_estimate=cost(2.0),
        name="moments",
    )(got, b, high, u, faces, acc)
    all_sums = lax.all_to_all(sums, "space", 0, 0)
    terms = pl.pallas_call(
        sense_kernel,
        out_shape=shape(N_FREQ, DEPTH, 128),
        in_specs=[smem()] + [vmem()] * 3,
        out_specs=vmem(),
        compiler_params=params(),
        cost_estimate=cost(1.0),
        name="sensitivity",
    )(frequency, all_sums, products, sigma)
    shared = lax.all_to_all(terms, "freq", 0, 0)
    x, sampled = pl.pallas_call(
        field_kernel,
        out_shape=(shape(2, 2, 3, PLANES, DEPTH, WIDTH), shape(2, 2, 3, stations)),
        in_specs=[smem()] + [vmem()] * 6,
        out_specs=(vmem(),) * 2,
        compiler_params=params(),
        cost_estimate=cost(3.0),
        name="field",
    )(frequency, all_sums, b, u, sigma, station_cells[None], station_depth[None])
    gradient = pl.pallas_call(
        gradient_kernel,
        out_shape=shape(PLANES, DEPTH, SLAB),
        in_specs=[vmem()] * 2,
        out_specs=vmem(),
        compiler_params=params(),
        name="gradient",
    )(shared, conductivity)
    return x[None], sampled[None], gradient


def solution(mesh):
    return jax.shard_map(
        local,
        mesh=mesh,
        in_specs=(
            P("freq", None, None, None, "space", None, None),
            P("space", None, "freq"),
            P("freq"),
            P("space"),
            P("space"),
        ),
        out_specs=(
            P("freq", None, None, None, "space", None, None),
            P("freq", None, None, None, "space"),
            P("space", None, "freq"),
        ),
        check_vma=False,
    )
```

```python
import functools
import jax
import jax.numpy as jnp
from jax import lax
from jax.experimental import pallas as pl
from jax.experimental.pallas import tpu as pltpu
from jax.sharding import PartitionSpec as P

F32 = jnp.float32
N_FREQ = 8
N_SPACE = 32
DEPTH = 16
WIDTH = 256
PLANES = 4
SLAB = WIDTH // N_FREQ
LIMIT = 24 * 1024 * 1024


def params():
    return pltpu.CompilerParams(vmem_limit_bytes=LIMIT)


def vmem():
    return pl.BlockSpec(memory_space=pltpu.VMEM)


def anywhere():
    return pl.BlockSpec(memory_space=pl.ANY)


def smem():
    return pl.BlockSpec(memory_space=pltpu.SMEM)


def iota(dim, shape=(DEPTH, WIDTH)):
    return lax.broadcasted_iota(jnp.int32, shape, dim)


class Stencil:
    def __init__(self):
        row, lane = iota(0), iota(1)
        self.first_row, self.last_row = row == 0, row == DEPTH - 1
        self.first_lane, self.last_lane = lane == 0, lane == WIDTH - 1

    def fy(self, f):
        return jnp.where(self.last_lane, 0.0, pltpu.roll(f, WIDTH - 1, 1)) - f

    def fz(self, f):
        return jnp.where(self.last_row, 0.0, pltpu.roll(f, DEPTH - 1, 0)) - f

    def by(self, g, before):
        return g - jnp.where(self.first_lane, before, pltpu.roll(g, 1, 1))

    def bz(self, g, before):
        return g - jnp.where(self.first_row, before, pltpu.roll(g, 1, 0))

    def faces_yz(self, ex, ey, ez, ey_next, ez_next):
        return self.fz(ex) - (ez_next - ez), (ey_next - ey) - self.fy(ex)

    def face_x(self, ey, ez):
        return self.fy(ez) - self.fz(ey)

    def edge_terms(self, px, py, pz):
        return jnp.where(self.first_lane, px + pz, 0.0) + jnp.where(self.first_row, px + py, 0.0)


def fold(plane):
    half = plane[:8] + plane[8:]
    return half[:, :128] + half[:, 128:]


def dot3(a, b):
    return a[0] * b[0] + a[1] * b[1] + a[2] * b[2]


LAST = PLANES - 1
SLAB_PLANE = 16


def send_kernel(b_ref, own_ref, left_ref, right_ref):
    st = Stencil()
    for pol in range(2):
        for part in range(2):
            k = 2 * pol + part
            ex, ey, ez = [b_ref[pol, part, c, 0] for c in range(3)]
            hx = st.face_x(ey, ez)
            hy, hz = st.faces_yz(ex, ey, ez, b_ref[pol, part, 1, 1], b_ref[pol, part, 2, 1])
            left_ref[4 * k] = ey
            left_ref[4 * k + 1] = ez
            left_ref[4 * k + 2] = st.bz(hx, -ey) - hz
            left_ref[4 * k + 3] = hy - st.by(hx, ez)
            ex, ey, ez = [b_ref[pol, part, c, LAST] for c in range(3)]
            right_ref[2 * k] = st.fz(ex) + ez
            right_ref[2 * k + 1] = -ey - st.fy(ex)
    front = jnp.concatenate([own_ref[0]] * 4, axis=1)
    left_ref[SLAB_PLANE] = jnp.concatenate([front, front], axis=1)


def pack_kernel(own_ref, high_ref, out_ref):
    own = jnp.concatenate([own_ref[i] for i in range(PLANES)], axis=1)
    for f in range(N_FREQ):
        out_ref[f, 0] = own
        out_ref[f, 1] = high_ref[SLAB_PLANE, :, :128]


def curl_kernel(b_ref, low_ref, high_ref, u_ref, face_ref, t_ref, acc_ref):
    st = Stencil()
    place = lax.axis_index("space")
    keep_next = jnp.where(place == N_SPACE - 1, 0.0, 1.0).astype(F32)
    is_first = jnp.where(place == 0, 1.0, 0.0).astype(F32)

    def one_pol(pol, carry):
        s0 = jnp.zeros((8, 128), F32)
        s1 = jnp.zeros((8, 128), F32)
        s2 = jnp.zeros((8, 128), F32)
        s3 = jnp.zeros((8, 128), F32)
        for part in range(2):
            k = 2 * pol + part

            def field(c, i):
                return b_ref[pol, part, c, i] if i < PLANES else high_ref[4 * k + c - 1]

            hy_old = low_ref[2 * k] - field(2, 0)
            hz_old = low_ref[2 * k + 1] + field(1, 0)
            u_old = None
            for i in range(PLANES + 1):
                if i < PLANES:
                    ex, ey, ez = field(0, i), field(1, i), field(2, i)
                    hx = st.face_x(ey, ez)
                    hy, hz = st.faces_yz(ex, ey, ez, field(1, i + 1), field(2, i + 1))
                    uy = st.bz(hx, -ey) - (hz - hz_old)
                    uz = (hy - hy_old) - st.by(hx, ez)
                    hy_old, hz_old = hy, hz
                    ux = st.by(hz, -ex) - st.bz(hy, ex)
                    u_ref[pol, part, 0, i] = ux
                    u_ref[pol, part, 1, i] = uy
                    u_ref[pol, part, 2, i] = uz
                    s0 = s0 + fold(ex * ex + ey * ey + ez * ez)
                    s1 = s1 + fold(ex * ux + ey * uy + ez * uz)
                else:
                    uy = keep_next * (high_ref[4 * k + 2] + hz_old)
                    uz = keep_next * (high_ref[4 * k + 3] - hy_old)
                if u_old is not None:
                    px, py, pz = u_old
                    fx = st.face_x(py, pz)
                    fy, fz = st.faces_yz(px, py, pz, uy, uz)
                    face_ref[pol, part, 0, i - 1] = fx
                    face_ref[pol, part, 1, i - 1] = fy
                    face_ref[pol, part, 2, i - 1] = fz
                    qx, qy, qz = px * px, py * py, pz * pz
                    s2 = s2 + fold(qx + qy + qz)
                    total = fx * fx + fy * fy + fz * fz + st.edge_terms(qx, qy, qz)
                    if i == 1:
                        total = total + is_first * (qy + qz)
                    s3 = s3 + fold(total)
                if i < PLANES:
                    u_old = (ux, uy, uz)
        acc_ref[pol, 0] = s0
        acc_ref[pol, 1] = s1
        acc_ref[pol, 2] = s2
        acc_ref[pol, 3] = s3
        for i in range(PLANES):
            br = [b_ref[pol, 0, c, i] for c in range(3)]
            bi = [b_ref[pol, 1, c, i] for c in range(3)]
            ur = [u_ref[pol, 0, c, i] for c in range(3)]
            ui = [u_ref[pol, 1, c, i] for c in range(3)]
            t_ref[pol, 0, i] = dot3(br, br) - dot3(bi, bi)
            t_ref[pol, 1, i] = dot3(ur, ur) - dot3(ui, ui)
            t_ref[pol, 2, i] = dot3(br, ur) - dot3(bi, ui)
        return carry

    lax.fori_loop(0, 2, one_pol, 0)


N_SUMS = 12


def moment_kernel(got_ref, b_ref, high_ref, u_ref, face_ref, acc_ref, sigma_ref, sums_ref, next_ref):
    st = Stencil()
    is_first = jnp.where(lax.axis_index("space") == 0, 1.0, 0.0).astype(F32)
    group = iota(1, (DEPTH, 128)) // SLAB
    for half in range(2):
        cols = pl.ds(128 * half, 128)
        for i in range(PLANES + 1):
            value = None
            for q in range(4):
                piece = got_ref[4 * half + q, 0 if i < PLANES else 1]
                shift = (SLAB * (q - i)) % 128 if i < PLANES else 0
                piece = pltpu.roll(piece, shift, 1) if shift else piece
                value = piece if value is None else jnp.where(group == q, piece, value)
            if i < PLANES:
                sigma_ref[i, :, cols] = value
            else:
                next_ref[:, cols] = value

    lane = iota(1, (1, 128))

    def one_pol(pol, row):
        names = ("d1", "d2", "d3", "e1", "e2", "g", "x1", "x2")
        acc = {name: jnp.zeros((8, 128), F32) for name in names}

        def add(name, plane):
            acc[name] = acc[name] + fold(plane)

        for part in range(2):
            after = next_ref[...]
            wy_next = after * high_ref[4 * (2 * pol + part)]
            wz_next = after * high_ref[4 * (2 * pol + part) + 1]
            for i in reversed(range(PLANES)):
                s = sigma_ref[i]
                b = [b_ref[pol, part, c, i] for c in range(3)]
                u = [u_ref[pol, part, c, i] for c in range(3)]
                w = [s * f for f in b]
                fx = st.face_x(w[1], w[2])
                fy, fz = st.faces_yz(w[0], w[1], w[2], wy_next, wz_next)
                wy_next, wz_next = w[1], w[2]
                gx, gy, gz = [face_ref[pol, part, c, i] for c in range(3)]
                rx, ry, rz = [f * f for f in w]
                qx, qy, qz = [f * v for f, v in zip(w, u)]
                ww = rx + ry + rz
                uw = qx + qy + qz
                x1 = fx * gx + fy * gy + fz * gz + st.edge_terms(qx, qy, qz)
                x2 = fx * fx + fy * fy + fz * fz + st.edge_terms(rx, ry, rz)
                if i == 0:
                    x1 = x1 + is_first * (qy + qz)
                    x2 = x2 + is_first * (ry + rz)
                add("x1", x1)
                add("x2", x2)
                add("d1", dot3(w, b))
                add("d2", ww)
                add("d3", s * ww)
                add("e1", uw)
                add("e2", s * dot3(u, u))
                add("g", s * uw)
        every = [acc_ref[pol, k] for k in range(4)] + [acc[name] for name in names]
        for k, value in enumerate(every):
            row = row + jnp.where(lane == k + 64 * pol, jnp.sum(value, axis=(0, 1), keepdims=True), 0.0)
        return row

    row = lax.fori_loop(0, 2, one_pol, jnp.zeros((1, 128), F32))
    for k in range(N_SPACE):
        sums_ref[k] = row


def times(a, b):
    return a[0] * b[0] - a[1] * b[1], a[0] * b[1] + a[1] * b[0]


def over(a, b):
    denom = b[0] * b[0] + b[1] * b[1]
    return (a[0] * b[0] + a[1] * b[1]) / denom, (a[1] * b[0] - a[0] * b[1]) / denom


def steps(sums_ref, omega):
    row = jnp.sum(jnp.concatenate([sums_ref[k] for k in range(N_SPACE)], axis=0), axis=0, keepdims=True)
    found = []
    for pol in range(2):
        s0, s1, s2, s3, d1, d2, d3, e1, e2, g, x1, x2 = [
            row[:, k + 64 * pol : k + 64 * pol + 1] for k in range(N_SUMS)
        ]
        w2 = omega * omega
        m0 = (s0, jnp.zeros_like(s0))
        m1 = (s1, omega * d1)
        m2 = (s2 - w2 * d2, 2.0 * omega * e1)
        m3 = (s3 - w2 * (2.0 * g + x2), omega * (2.0 * x1 + e2) - omega * w2 * d3)
        a0 = over(m0, m1)
        a0a0 = times(a0, a0)
        z = times(a0a0, m2)
        rho = (z[0] - s0, z[1])
        grow = (1.0 + rho[0] / s0, rho[1] / s0)
        first = times(times(grow, grow), m1)
        second = times(times(a0, grow), m2)
        third = times(a0a0, m3)
        curv = (first[0] - 2.0 * second[0] + third[0], first[1] - 2.0 * second[1] + third[1])
        a1 = over(rho, curv)
        a1g = times(a1, grow)
        a1a0 = times(a1, a0)
        found.append(((a0[0] + a1g[0], a0[1] + a1g[1]), (-a1a0[0], -a1a0[1])))
    return found


def sense_kernel(omega_ref, sums_ref, t_ref, sigma_ref, out_ref):
    omega = omega_ref[0]
    found = steps(sums_ref, omega)
    group = iota(1, (DEPTH, 128)) // SLAB
    planes = []
    for i in range(PLANES):
        scaled = omega * sigma_ref[i]
        total = jnp.zeros((DEPTH, WIDTH), F32)
        for pol in range(2):
            c0, c1 = found[pol]
            fr = c0[0] - scaled * c1[1]
            fi = c0[1] + scaled * c1[0]
            total = total + (fr * fr + fi * fi) * t_ref[pol, 0, i]
            total = total + (c1[0] * c1[0] + c1[1] * c1[1]) * t_ref[pol, 1, i]
            total = total + 2.0 * (fr * c1[0] + fi * c1[1]) * t_ref[pol, 2, i]
        planes.append(omega * total)
    for f in range(N_FREQ):
        half, q = f // 4, f % 4
        value = None
        for i in range(PLANES):
            piece = planes[i][:, 128 * half : 128 * half + 128]
            shift = (SLAB * (i - q)) % 128
            piece = pltpu.roll(piece, shift, 1) if shift else piece
            value = piece if value is None else jnp.where(group == i, piece, value)
        out_ref[f] = value


def field_kernel(omega_ref, sums_ref, b_ref, u_ref, sigma_ref, cells_ref, depth_ref, x_ref, sampled_ref):
    omega = omega_ref[0]
    found = steps(sums_ref, omega)
    cells, depth = cells_ref[...], depth_ref[...]
    stations = cells.shape[1]
    in_row = iota(0, (PLANES * DEPTH, stations)) == cells // WIDTH * DEPTH + depth
    in_lane = (iota(0, (WIDTH, stations)) == cells % WIDTH).astype(F32)
    for pol in range(2):
        c0, c1 = found[pol]
        for i in range(PLANES):
            scaled = omega * sigma_ref[i]
            fr = c0[0] - scaled * c1[1]
            fi = c0[1] + scaled * c1[0]
            for c in range(3):
                br, bi = b_ref[pol, 0, c, i], b_ref[pol, 1, c, i]
                ur, ui = u_ref[pol, 0, c, i], u_ref[pol, 1, c, i]
                x_ref[pol, 0, c, i] = fr * br - fi * bi + c1[0] * ur - c1[1] * ui
                x_ref[pol, 1, c, i] = fr * bi + fi * br + c1[0] * ui + c1[1] * ur
        for part in range(2):
            for c in range(3):
                rows = x_ref[pol, part, c].reshape(PLANES * DEPTH, WIDTH)
                picked = jnp.dot(rows, in_lane, precision=lax.Precision.HIGHEST, preferred_element_type=F32)
                sampled_ref[pol, part, pl.ds(c, 1)] = jnp.sum(
                    jnp.where(in_row, picked, 0.0), axis=0, keepdims=True
                )


def gradient_kernel(terms_ref, own_ref, out_ref):
    total = terms_ref[0]
    for f in range(1, N_FREQ):
        total = total + terms_ref[f]
    for i in range(PLANES):
        out_ref[i] = own_ref[i] * total[:, SLAB * i : SLAB * i + SLAB] * (1.0 / (3.0 * 2 * N_FREQ))


def shape(*dims):
    return jax.ShapeDtypeStruct(dims, F32)


def cost(us):
    return pl.CostEstimate(flops=int(us * 1.0e9), bytes_accessed=int(us * 3.0e6), transcendentals=0)


def local(source_current, conductivity, frequency, station_cells, station_depth):
    b = source_current[0]
    stations = station_cells.shape[0]
    ends = N_SPACE - 1
    upward = [(i, i + 1) for i in range(ends)]
    downward = [(i + 1, i) for i in range(ends)]

    to_left, to_right = pl.pallas_call(
        send_kernel,
        out_shape=(shape(SLAB_PLANE + 1, DEPTH, WIDTH), shape(8, DEPTH, WIDTH)),
        in_specs=[vmem(), vmem()],
        out_specs=(vmem(), vmem()),
        compiler_params=params(),
        name="edge_planes",
    )(b, conductivity)
    high = lax.ppermute(to_left, "space", downward)
    low = lax.ppermute(to_right, "space", upward)
    packed = pl.pallas_call(
        pack_kernel,
        out_shape=shape(N_FREQ, 2, DEPTH, 128),
        in_specs=[vmem(), vmem()],
        out_specs=vmem(),
        compiler_params=params(),
        name="pack_conductivity",
    )(conductivity, high)
    got = lax.all_to_all(packed, "freq", 0, 0)

    u, faces, products, acc = pl.pallas_call(
        curl_kernel,
        out_shape=(
            shape(2, 2, 3, PLANES, DEPTH, WIDTH),
            shape(2, 2, 3, PLANES, DEPTH, WIDTH),
            shape(2, 3, PLANES, DEPTH, WIDTH),
            shape(2, 4, 8, 128),
        ),
        in_specs=[vmem()] * 3,
        out_specs=(vmem(),) * 4,
        compiler_params=params(),
        cost_estimate=cost(3.0),
        name="curl_curl",
    )(b, low, high)
    sigma, sums = pl.pallas_call(
        moment_kernel,
        out_shape=(shape(PLANES, DEPTH, WIDTH), shape(N_SPACE, 1, 128)),
        in_specs=[vmem()] * 6,
        out_specs=(vmem(),) * 2,
        scratch_shapes=[pltpu.VMEM((DEPTH, WIDTH), F32)],
        compiler_params=params(),
        cost_estimate=cost(2.0),
        name="moments",
    )(got, b, high, u, faces, acc)
    all_sums = lax.all_to_all(sums, "space", 0, 0)
    terms = pl.pallas_call(
        sense_kernel,
        out_shape=shape(N_FREQ, DEPTH, 128),
        in_specs=[smem()] + [vmem()] * 3,
        out_specs=vmem(),
        compiler_params=params(),
        cost_estimate=cost(1.0),
        name="sensitivity",
    )(frequency, all_sums, products, sigma)
    shared = lax.all_to_all(terms, "freq", 0, 0)
    x, sampled = pl.pallas_call(
        field_kernel,
        out_shape=(shape(2, 2, 3, PLANES, DEPTH, WIDTH), shape(2, 2, 3, stations)),
        in_specs=[smem()] + [vmem()] * 6,
        out_specs=(vmem(),) * 2,
        compiler_params=params(),
        cost_estimate=cost(3.0),
        name="field",
    )(frequency, all_sums, b, u, sigma, station_cells[None], station_depth[None])
    gradient = pl.pallas_call(
        gradient_kernel,
        out_shape=shape(PLANES, DEPTH, SLAB),
        in_specs=[vmem()] * 2,
        out_specs=vmem(),
        compiler_params=params(),
        name="gradient",
    )(shared, conductivity)
    return x[None], sampled[None], gradient


def solution(mesh):
    return jax.shard_map(
        local,
        mesh=mesh,
        in_specs=(
            P("freq", None, None, None, "space", None, None),
            P("space", None, "freq"),
            P("freq"),
            P("space"),
            P("space"),
        ),
        out_specs=(
            P("freq", None, None, None, "space", None, None),
            P("freq", None, None, None, "space"),
            P("space", None, "freq"),
        ),
        check_vma=False,
    )
```

```python
import functools
import jax
import jax.numpy as jnp
from jax import lax
from jax.experimental import pallas as pl
from jax.experimental.pallas import tpu as pltpu
from jax.sharding import PartitionSpec as P

F32 = jnp.float32
N_FREQ = 8
N_SPACE = 32
DEPTH = 16
WIDTH = 256
PLANES = 4
SLAB = WIDTH // N_FREQ
LIMIT = 24 * 1024 * 1024


def params():
    return pltpu.CompilerParams(vmem_limit_bytes=LIMIT)


def vmem():
    return pl.BlockSpec(memory_space=pltpu.VMEM)


def anywhere():
    return pl.BlockSpec(memory_space=pl.ANY)


def smem():
    return pl.BlockSpec(memory_space=pltpu.SMEM)


def iota(dim, shape=(DEPTH, WIDTH)):
    return lax.broadcasted_iota(jnp.int32, shape, dim)


class Stencil:
    def __init__(self):
        row, lane = iota(0), iota(1)
        self.first_row, self.last_row = row == 0, row == DEPTH - 1
        self.first_lane, self.last_lane = lane == 0, lane == WIDTH - 1

    def fy(self, f):
        return jnp.where(self.last_lane, 0.0, pltpu.roll(f, WIDTH - 1, 1)) - f

    def fz(self, f):
        return jnp.where(self.last_row, 0.0, pltpu.roll(f, DEPTH - 1, 0)) - f

    def by(self, g, before):
        return g - jnp.where(self.first_lane, before, pltpu.roll(g, 1, 1))

    def bz(self, g, before):
        return g - jnp.where(self.first_row, before, pltpu.roll(g, 1, 0))

    def faces_yz(self, ex, ey, ez, ey_next, ez_next):
        return self.fz(ex) - (ez_next - ez), (ey_next - ey) - self.fy(ex)

    def face_x(self, ey, ez):
        return self.fy(ez) - self.fz(ey)

    def edge_terms(self, px, py, pz):
        return jnp.where(self.first_lane, px + pz, 0.0) + jnp.where(self.first_row, px + py, 0.0)


def fold(plane):
    half = plane[:8] + plane[8:]
    return half[:, :128] + half[:, 128:]


def dot3(a, b):
    return a[0] * b[0] + a[1] * b[1] + a[2] * b[2]


LAST = PLANES - 1
SLAB_PLANE = 16


def placed(parts, lanes):
    row, lane = iota(0, (8, 128)), iota(1, (8, 128))
    table = jnp.zeros((8, 128), F32)
    target = jnp.full((8, 128), -1, jnp.int32)
    for n, (part, at) in enumerate(zip(parts, lanes)):
        table = jnp.where(row == n, jnp.sum(part, axis=0, keepdims=True), table)
        target = jnp.where(row == n, at, target)
    totals = jnp.sum(table, axis=1, keepdims=True)
    return jnp.sum(jnp.where(lane == target, totals, 0.0), axis=0, keepdims=True)


def send_kernel(b_ref, own_ref, left_ref, right_ref):
    st = Stencil()
    for pol in range(2):
        for part in range(2):
            k = 2 * pol + part
            ex, ey, ez = [b_ref[pol, part, c, 0] for c in range(3)]
            hx = st.face_x(ey, ez)
            hy, hz = st.faces_yz(ex, ey, ez, b_ref[pol, part, 1, 1], b_ref[pol, part, 2, 1])
            left_ref[4 * k] = ey
            left_ref[4 * k + 1] = ez
            left_ref[4 * k + 2] = st.bz(hx, -ey) - hz
            left_ref[4 * k + 3] = hy - st.by(hx, ez)
            ex, ey, ez = [b_ref[pol, part, c, LAST] for c in range(3)]
            right_ref[2 * k] = st.fz(ex) + ez
            right_ref[2 * k + 1] = -ey - st.fy(ex)
    front = jnp.concatenate([own_ref[0]] * 4, axis=1)
    left_ref[SLAB_PLANE] = jnp.concatenate([front, front], axis=1)


def pack_kernel(own_ref, high_ref, out_ref):
    own = jnp.concatenate([own_ref[i] for i in range(PLANES)], axis=1)
    for f in range(N_FREQ):
        out_ref[f, 0] = own
        out_ref[f, 1] = high_ref[SLAB_PLANE, :, :128]


def curl_kernel(b_ref, low_ref, high_ref, u_ref, face_ref, t_ref, row_ref, keep_ref):
    st = Stencil()
    place = lax.axis_index("space")
    keep_next = jnp.where(place == N_SPACE - 1, 0.0, 1.0).astype(F32)
    is_first = jnp.where(place == 0, 1.0, 0.0).astype(F32)

    def one_pol(pol, carry):
        s0 = jnp.zeros((8, 128), F32)
        s1 = jnp.zeros((8, 128), F32)
        s2 = jnp.zeros((8, 128), F32)
        s3 = jnp.zeros((8, 128), F32)
        for part in range(2):
            k = 2 * pol + part

            def field(c, i):
                return b_ref[pol, part, c, i] if i < PLANES else high_ref[4 * k + c - 1]

            hy_old = low_ref[2 * k] - field(2, 0)
            hz_old = low_ref[2 * k + 1] + field(1, 0)
            u_old = None
            for i in range(PLANES + 1):
                if i < PLANES:
                    ex, ey, ez = field(0, i), field(1, i), field(2, i)
                    hx = st.face_x(ey, ez)
                    hy, hz = st.faces_yz(ex, ey, ez, field(1, i + 1), field(2, i + 1))
                    uy = st.bz(hx, -ey) - (hz - hz_old)
                    uz = (hy - hy_old) - st.by(hx, ez)
                    hy_old, hz_old = hy, hz
                    ux = st.by(hz, -ex) - st.bz(hy, ex)
                    u_ref[pol, part, 0, i] = ux
                    u_ref[pol, part, 1, i] = uy
                    u_ref[pol, part, 2, i] = uz
                    s0 = s0 + fold(ex * ex + ey * ey + ez * ez)
                    s1 = s1 + fold(ex * ux + ey * uy + ez * uz)
                else:
                    uy = keep_next * (high_ref[4 * k + 2] + hz_old)
                    uz = keep_next * (high_ref[4 * k + 3] - hy_old)
                if u_old is not None:
                    px, py, pz = u_old
                    fx = st.face_x(py, pz)
                    fy, fz = st.faces_yz(px, py, pz, uy, uz)
                    face_ref[pol, part, 0, i - 1] = fx
                    face_ref[pol, part, 1, i - 1] = fy
                    face_ref[pol, part, 2, i - 1] = fz
                    qx, qy, qz = px * px, py * py, pz * pz
                    s2 = s2 + fold(qx + qy + qz)
                    total = fx * fx + fy * fy + fz * fz + st.edge_terms(qx, qy, qz)
                    if i == 1:
                        total = total + is_first * (qy + qz)
                    s3 = s3 + fold(total)
                if i < PLANES:
                    u_old = (ux, uy, uz)
        for n, value in enumerate((s0, s1, s2, s3)):
            keep_ref[4 * pol + n] = value
        for i in range(PLANES):
            br = [b_ref[pol, 0, c, i] for c in range(3)]
            bi = [b_ref[pol, 1, c, i] for c in range(3)]
            ur = [u_ref[pol, 0, c, i] for c in range(3)]
            ui = [u_ref[pol, 1, c, i] for c in range(3)]
            t_ref[pol, 0, i] = dot3(br, br) - dot3(bi, bi)
            t_ref[pol, 1, i] = dot3(ur, ur) - dot3(ui, ui)
            t_ref[pol, 2, i] = dot3(br, ur) - dot3(bi, ui)
        return carry

    lax.fori_loop(0, 2, one_pol, 0)
    row_ref[...] = placed([keep_ref[n] for n in range(8)], [n % 4 + 64 * (n // 4) for n in range(8)])


N_SUMS = 10


def moment_kernel(_, got_ref, b_ref, high_ref, u_ref, face_ref, row_ref, sigma_ref, sums_ref, next_ref, keep_ref):
    st = Stencil()
    is_first = jnp.where(lax.axis_index("space") == 0, 1.0, 0.0).astype(F32)
    group = iota(1, (DEPTH, 128)) // SLAB
    for half in range(2):
        cols = pl.ds(128 * half, 128)
        for i in range(PLANES + 1):
            value = None
            for q in range(4):
                piece = got_ref[4 * half + q, 0 if i < PLANES else 1]
                shift = (SLAB * (q - i)) % 128 if i < PLANES else 0
                piece = pltpu.roll(piece, shift, 1) if shift else piece
                value = piece if value is None else jnp.where(group == q, piece, value)
            if i < PLANES:
                sigma_ref[i, :, cols] = value
            else:
                next_ref[:, cols] = value

    def one_pol(pol, carry):
        names = ("d1", "d2", "d3", "e1", "re", "im")
        acc = {name: jnp.zeros((8, 128), F32) for name in names}

        def add(name, plane):
            acc[name] = acc[name] + fold(plane)

        for part in range(2):
            after = next_ref[...]
            wy_next = after * high_ref[4 * (2 * pol + part)]
            wz_next = after * high_ref[4 * (2 * pol + part) + 1]
            for i in reversed(range(PLANES)):
                s = sigma_ref[i]
                b = [b_ref[pol, part, c, i] for c in range(3)]
                u = [u_ref[pol, part, c, i] for c in range(3)]
                w = [s * f for f in b]
                fx = st.face_x(w[1], w[2])
                fy, fz = st.faces_yz(w[0], w[1], w[2], wy_next, wz_next)
                wy_next, wz_next = w[1], w[2]
                gx, gy, gz = [face_ref[pol, part, c, i] for c in range(3)]
                rx, ry, rz = [f * f for f in w]
                qx, qy, qz = [f * v for f, v in zip(w, u)]
                ww = rx + ry + rz
                uw = qx + qy + qz
                x1 = fx * gx + fy * gy + fz * gz + st.edge_terms(qx, qy, qz)
                x2 = fx * fx + fy * fy + fz * fz + st.edge_terms(rx, ry, rz)
                if i == 0:
                    x1 = x1 + is_first * (qy + qz)
                    x2 = x2 + is_first * (ry + rz)
                add("d1", dot3(w, b))
                add("d2", ww)
                add("d3", s * ww)
                add("e1", uw)
                add("re", x2 + 2.0 * s * uw)
                add("im", 2.0 * x1 + s * dot3(u, u))
        for n, name in enumerate(names):
            keep_ref[pol, n] = acc[name]
        return carry

    lax.fori_loop(0, 2, one_pol, 0)
    row = row_ref[...]
    for pol in range(2):
        row = row + placed([keep_ref[pol, n] for n in range(6)], [64 * pol + 4 + n for n in range(6)])
    for k in range(N_SPACE):
        sums_ref[k] = row


def times(a, b):
    return a[0] * b[0] - a[1] * b[1], a[0] * b[1] + a[1] * b[0]


def over(a, b):
    denom = b[0] * b[0] + b[1] * b[1]
    return (a[0] * b[0] + a[1] * b[1]) / denom, (a[1] * b[0] - a[0] * b[1]) / denom


def steps(sums_ref, omega):
    row = jnp.sum(jnp.concatenate([sums_ref[k] for k in range(N_SPACE)], axis=0), axis=0, keepdims=True)
    found = []
    for pol in range(2):
        s0, s1, s2, s3, d1, d2, d3, e1, re, im = [
            row[:, k + 64 * pol : k + 64 * pol + 1] for k in range(N_SUMS)
        ]
        w2 = omega * omega
        m0 = (s0, jnp.zeros_like(s0))
        m1 = (s1, omega * d1)
        m2 = (s2 - w2 * d2, 2.0 * omega * e1)
        m3 = (s3 - w2 * re, omega * im - omega * w2 * d3)
        a0 = over(m0, m1)
        a0a0 = times(a0, a0)
        z = times(a0a0, m2)
        rho = (z[0] - s0, z[1])
        grow = (1.0 + rho[0] / s0, rho[1] / s0)
        first = times(times(grow, grow), m1)
        second = times(times(a0, grow), m2)
        third = times(a0a0, m3)
        curv = (first[0] - 2.0 * second[0] + third[0], first[1] - 2.0 * second[1] + third[1])
        a1 = over(rho, curv)
        a1g = times(a1, grow)
        a1a0 = times(a1, a0)
        found.append(((a0[0] + a1g[0], a0[1] + a1g[1]), (-a1a0[0], -a1a0[1])))
    return found


def sense_kernel(omega_ref, sums_ref, t_ref, sigma_ref, out_ref):
    omega = omega_ref[0]
    found = steps(sums_ref, omega)
    group = iota(1, (DEPTH, 128)) // SLAB
    planes = []
    for i in range(PLANES):
        scaled = omega * sigma_ref[i]
        total = jnp.zeros((DEPTH, WIDTH), F32)
        for pol in range(2):
            c0, c1 = found[pol]
            fr = c0[0] - scaled * c1[1]
            fi = c0[1] + scaled * c1[0]
            total = total + (fr * fr + fi * fi) * t_ref[pol, 0, i]
            total = total + (c1[0] * c1[0] + c1[1] * c1[1]) * t_ref[pol, 1, i]
            total = total + 2.0 * (fr * c1[0] + fi * c1[1]) * t_ref[pol, 2, i]
        planes.append(omega * total)
    for f in range(N_FREQ):
        half, q = f // 4, f % 4
        value = None
        for i in range(PLANES):
            piece = planes[i][:, 128 * half : 128 * half + 128]
            shift = (SLAB * (i - q)) % 128
            piece = pltpu.roll(piece, shift, 1) if shift else piece
            value = piece if value is None else jnp.where(group == i, piece, value)
        out_ref[f] = value


def field_kernel(omega_ref, sums_ref, b_ref, u_ref, sigma_ref, cells_ref, depth_ref, x_ref, sampled_ref):
    omega = omega_ref[0]
    found = steps(sums_ref, omega)
    cells, depth = cells_ref[...], depth_ref[...]
    stations = cells.shape[1]
    in_row = iota(0, (PLANES * DEPTH, stations)) == cells // WIDTH * DEPTH + depth
    in_lane = (iota(0, (WIDTH, stations)) == cells % WIDTH).astype(F32)
    for pol in range(2):
        c0, c1 = found[pol]
        for i in range(PLANES):
            scaled = omega * sigma_ref[i]
            fr = c0[0] - scaled * c1[1]
            fi = c0[1] + scaled * c1[0]
            for c in range(3):
                br, bi = b_ref[pol, 0, c, i], b_ref[pol, 1, c, i]
                ur, ui = u_ref[pol, 0, c, i], u_ref[pol, 1, c, i]
                x_ref[pol, 0, c, i] = fr * br - fi * bi + c1[0] * ur - c1[1] * ui
                x_ref[pol, 1, c, i] = fr * bi + fi * br + c1[0] * ui + c1[1] * ur
        for part in range(2):
            for c in range(3):
                rows = x_ref[pol, part, c].reshape(PLANES * DEPTH, WIDTH)
                picked = jnp.dot(rows, in_lane, precision=lax.Precision.HIGHEST, preferred_element_type=F32)
                sampled_ref[pol, part, pl.ds(c, 1)] = jnp.sum(
                    jnp.where(in_row, picked, 0.0), axis=0, keepdims=True
                )


def gradient_kernel(terms_ref, own_ref, out_ref):
    total = terms_ref[0]
    for f in range(1, N_FREQ):
        total = total + terms_ref[f]
    for i in range(PLANES):
        out_ref[i] = own_ref[i] * total[:, SLAB * i : SLAB * i + SLAB] * (1.0 / (3.0 * 2 * N_FREQ))


def shape(*dims):
    return jax.ShapeDtypeStruct(dims, F32)


def cost(us):
    return pl.CostEstimate(flops=int(us * 1.0e9), bytes_accessed=int(us * 3.0e6), transcendentals=0)


def local(source_current, conductivity, frequency, station_cells, station_depth):
    b = source_current[0]
    stations = station_cells.shape[0]
    ends = N_SPACE - 1
    upward = [(i, i + 1) for i in range(ends)]
    downward = [(i + 1, i) for i in range(ends)]

    to_left, to_right = pl.pallas_call(
        send_kernel,
        out_shape=(shape(SLAB_PLANE + 1, DEPTH, WIDTH), shape(8, DEPTH, WIDTH)),
        in_specs=[vmem(), vmem()],
        out_specs=(vmem(), vmem()),
        compiler_params=params(),
        name="edge_planes",
    )(b, conductivity)
    high = lax.ppermute(to_left, "space", downward)
    low = lax.ppermute(to_right, "space", upward)
    packed = pl.pallas_call(
        pack_kernel,
        out_shape=shape(N_FREQ, 2, DEPTH, 128),
        in_specs=[vmem(), vmem()],
        out_specs=vmem(),
        compiler_params=params(),
        name="pack_conductivity",
    )(conductivity, high)
    got = lax.all_to_all(packed, "freq", 0, 0)

    u, faces, products, acc = pl.pallas_call(
        curl_kernel,
        out_shape=(
            shape(2, 2, 3, PLANES, DEPTH, WIDTH),
            shape(2, 2, 3, PLANES, DEPTH, WIDTH),
            shape(2, 3, PLANES, DEPTH, WIDTH),
            shape(1, 128),
        ),
        in_specs=[vmem()] * 3,
        out_specs=(vmem(),) * 4,
        scratch_shapes=[pltpu.VMEM((8, 8, 128), F32)],
        compiler_params=params(),
        cost_estimate=cost(3.0),
        name="curl_curl",
    )(b, low, high)
    sigma, sums = pl.pallas_call(
        moment_kernel,
        out_shape=(shape(PLANES, DEPTH, WIDTH), shape(N_SPACE, 1, 128)),
        in_specs=[smem()] + [vmem()] * 6,
        out_specs=(vmem(),) * 2,
        scratch_shapes=[pltpu.VMEM((DEPTH, WIDTH), F32), pltpu.VMEM((2, 6, 8, 128), F32)],
        compiler_params=params(),
        cost_estimate=cost(2.0),
        name="moments",
    )(frequency, got, b, high, u, faces, acc)
    all_sums = lax.all_to_all(sums, "space", 0, 0)
    terms = pl.pallas_call(
        sense_kernel,
        out_shape=shape(N_FREQ, DEPTH, 128),
        in_specs=[smem()] + [vmem()] * 3,
        out_specs=vmem(),
        compiler_params=params(),
        cost_estimate=cost(1.0),
        name="sensitivity",
    )(frequency, all_sums, products, sigma)
    shared = lax.all_to_all(terms, "freq", 0, 0)
    x, sampled = pl.pallas_call(
        field_kernel,
        out_shape=(shape(2, 2, 3, PLANES, DEPTH, WIDTH), shape(2, 2, 3, stations)),
        in_specs=[smem()] + [vmem()] * 6,
        out_specs=(vmem(),) * 2,
        compiler_params=params(),
        cost_estimate=cost(3.0),
        name="field",
    )(frequency, all_sums, b, u, sigma, station_cells[None], station_depth[None])
    gradient = pl.pallas_call(
        gradient_kernel,
        out_shape=shape(PLANES, DEPTH, SLAB),
        in_specs=[vmem()] * 2,
        out_specs=vmem(),
        compiler_params=params(),
        name="gradient",
    )(shared, conductivity)
    return x[None], sampled[None], gradient


def solution(mesh):
    return jax.shard_map(
        local,
        mesh=mesh,
        in_specs=(
            P("freq", None, None, None, "space", None, None),
            P("space", None, "freq"),
            P("freq"),
            P("space"),
            P("space"),
        ),
        out_specs=(
            P("freq", None, None, None, "space", None, None),
            P("freq", None, None, None, "space"),
            P("space", None, "freq"),
        ),
        check_vma=False,
    )
```

```python
import functools
import jax
import jax.numpy as jnp
from jax import lax
from jax.experimental import pallas as pl
from jax.experimental.pallas import tpu as pltpu
from jax.sharding import PartitionSpec as P

F32 = jnp.float32
N_FREQ = 8
N_SPACE = 32
DEPTH = 16
WIDTH = 256
PLANES = 4
SLAB = WIDTH // N_FREQ
LIMIT = 24 * 1024 * 1024


def params():
    return pltpu.CompilerParams(vmem_limit_bytes=LIMIT)


def vmem():
    return pl.BlockSpec(memory_space=pltpu.VMEM)


def anywhere():
    return pl.BlockSpec(memory_space=pl.ANY)


def smem():
    return pl.BlockSpec(memory_space=pltpu.SMEM)


def iota(dim, shape=(DEPTH, WIDTH)):
    return lax.broadcasted_iota(jnp.int32, shape, dim)


class Stencil:
    def __init__(self):
        row, lane = iota(0), iota(1)
        self.first_row, self.last_row = row == 0, row == DEPTH - 1
        self.first_lane, self.last_lane = lane == 0, lane == WIDTH - 1

    def fy(self, f):
        return jnp.where(self.last_lane, 0.0, pltpu.roll(f, WIDTH - 1, 1)) - f

    def fz(self, f):
        return jnp.where(self.last_row, 0.0, pltpu.roll(f, DEPTH - 1, 0)) - f

    def by(self, g, before):
        return g - jnp.where(self.first_lane, before, pltpu.roll(g, 1, 1))

    def bz(self, g, before):
        return g - jnp.where(self.first_row, before, pltpu.roll(g, 1, 0))

    def faces_yz(self, ex, ey, ez, ey_next, ez_next):
        return self.fz(ex) - (ez_next - ez), (ey_next - ey) - self.fy(ex)

    def face_x(self, ey, ez):
        return self.fy(ez) - self.fz(ey)

    def edge_terms(self, px, py, pz):
        return jnp.where(self.first_lane, px + pz, 0.0) + jnp.where(self.first_row, px + py, 0.0)


def fold(plane):
    half = plane[:8] + plane[8:]
    return half[:, :128] + half[:, 128:]


def dot3(a, b):
    return a[0] * b[0] + a[1] * b[1] + a[2] * b[2]


LAST = PLANES - 1
SLAB_PLANE = 16


def placed(parts, lanes):
    row, lane = iota(0, (8, 128)), iota(1, (8, 128))
    table = jnp.zeros((8, 128), F32)
    target = jnp.full((8, 128), -1, jnp.int32)
    for n, (part, at) in enumerate(zip(parts, lanes)):
        table = jnp.where(row == n, jnp.sum(part, axis=0, keepdims=True), table)
        target = jnp.where(row == n, at, target)
    totals = jnp.sum(table, axis=1, keepdims=True)
    return jnp.sum(jnp.where(lane == target, totals, 0.0), axis=0, keepdims=True)


def send_kernel(b_ref, sigma_ref, left_ref, right_ref, front_ref, second_ref, last_ref, own_ref, sems):
    copies = [
        pltpu.make_async_copy(b_ref.at[:, :, :, 0], front_ref, sems.at[0]),
        pltpu.make_async_copy(b_ref.at[:, :, pl.ds(1, 2), 1], second_ref, sems.at[1]),
        pltpu.make_async_copy(b_ref.at[:, :, :, LAST], last_ref, sems.at[2]),
        pltpu.make_async_copy(sigma_ref.at[pl.ds(0, 1)], own_ref, sems.at[3]),
    ]
    for copy in copies:
        copy.start()
    for copy in copies:
        copy.wait()
    st = Stencil()
    for pol in range(2):
        for part in range(2):
            k = 2 * pol + part
            ex, ey, ez = [front_ref[pol, part, c] for c in range(3)]
            hx = st.face_x(ey, ez)
            hy, hz = st.faces_yz(ex, ey, ez, second_ref[pol, part, 0], second_ref[pol, part, 1])
            left_ref[4 * k] = ey
            left_ref[4 * k + 1] = ez
            left_ref[4 * k + 2] = st.bz(hx, -ey) - hz
            left_ref[4 * k + 3] = hy - st.by(hx, ez)
            ex, ey, ez = [last_ref[pol, part, c] for c in range(3)]
            right_ref[2 * k] = st.fz(ex) + ez
            right_ref[2 * k + 1] = -ey - st.fy(ex)
    front = jnp.concatenate([own_ref[0]] * 4, axis=1)
    left_ref[SLAB_PLANE] = jnp.concatenate([front, front], axis=1)


def pack_kernel(own_ref, high_ref, out_ref):
    own = jnp.concatenate([own_ref[i] for i in range(PLANES)], axis=1)
    for f in range(N_FREQ):
        out_ref[f, 0] = own
        out_ref[f, 1] = high_ref[SLAB_PLANE, :, :128]


def curl_kernel(b_ref, low_ref, high_ref, u_ref, face_ref, t_ref, row_ref, keep_ref):
    st = Stencil()
    place = lax.axis_index("space")
    keep_next = jnp.where(place == N_SPACE - 1, 0.0, 1.0).astype(F32)
    is_first = jnp.where(place == 0, 1.0, 0.0).astype(F32)

    def one_pol(pol, carry):
        s0 = jnp.zeros((8, 128), F32)
        s1 = jnp.zeros((8, 128), F32)
        s2 = jnp.zeros((8, 128), F32)
        s3 = jnp.zeros((8, 128), F32)
        for part in range(2):
            k = 2 * pol + part

            def field(c, i):
                return b_ref[pol, part, c, i] if i < PLANES else high_ref[4 * k + c - 1]

            hy_old = low_ref[2 * k] - field(2, 0)
            hz_old = low_ref[2 * k + 1] + field(1, 0)
            u_old = None
            for i in range(PLANES + 1):
                if i < PLANES:
                    ex, ey, ez = field(0, i), field(1, i), field(2, i)
                    hx = st.face_x(ey, ez)
                    hy, hz = st.faces_yz(ex, ey, ez, field(1, i + 1), field(2, i + 1))
                    uy = st.bz(hx, -ey) - (hz - hz_old)
                    uz = (hy - hy_old) - st.by(hx, ez)
                    hy_old, hz_old = hy, hz
                    ux = st.by(hz, -ex) - st.bz(hy, ex)
                    u_ref[pol, part, 0, i] = ux
                    u_ref[pol, part, 1, i] = uy
                    u_ref[pol, part, 2, i] = uz
                    s0 = s0 + fold(ex * ex + ey * ey + ez * ez)
                    s1 = s1 + fold(ex * ux + ey * uy + ez * uz)
                else:
                    uy = keep_next * (high_ref[4 * k + 2] + hz_old)
                    uz = keep_next * (high_ref[4 * k + 3] - hy_old)
                if u_old is not None:
                    px, py, pz = u_old
                    fx = st.face_x(py, pz)
                    fy, fz = st.faces_yz(px, py, pz, uy, uz)
                    face_ref[pol, part, 0, i - 1] = fx
                    face_ref[pol, part, 1, i - 1] = fy
                    face_ref[pol, part, 2, i - 1] = fz
                    qx, qy, qz = px * px, py * py, pz * pz
                    s2 = s2 + fold(qx + qy + qz)
                    total = fx * fx + fy * fy + fz * fz + st.edge_terms(qx, qy, qz)
                    if i == 1:
                        total = total + is_first * (qy + qz)
                    s3 = s3 + fold(total)
                if i < PLANES:
                    u_old = (ux, uy, uz)
        for n, value in enumerate((s0, s1, s2, s3)):
            keep_ref[4 * pol + n] = value
        for i in range(PLANES):
            br = [b_ref[pol, 0, c, i] for c in range(3)]
            bi = [b_ref[pol, 1, c, i] for c in range(3)]
            ur = [u_ref[pol, 0, c, i] for c in range(3)]
            ui = [u_ref[pol, 1, c, i] for c in range(3)]
            t_ref[pol, 0, i] = dot3(br, br) - dot3(bi, bi)
            t_ref[pol, 1, i] = dot3(ur, ur) - dot3(ui, ui)
            t_ref[pol, 2, i] = dot3(br, ur) - dot3(bi, ui)
        return carry

    lax.fori_loop(0, 2, one_pol, 0)
    row_ref[...] = placed([keep_ref[n] for n in range(8)], [n % 4 + 64 * (n // 4) for n in range(8)])


N_SUMS = 10


def moment_kernel(_, got_ref, b_ref, high_ref, u_ref, face_ref, row_ref, sigma_ref, sums_ref, next_ref, keep_ref):
    st = Stencil()
    is_first = jnp.where(lax.axis_index("space") == 0, 1.0, 0.0).astype(F32)
    group = iota(1, (DEPTH, 128)) // SLAB
    for half in range(2):
        cols = pl.ds(128 * half, 128)
        for i in range(PLANES + 1):
            value = None
            for q in range(4):
                piece = got_ref[4 * half + q, 0 if i < PLANES else 1]
                shift = (SLAB * (q - i)) % 128 if i < PLANES else 0
                piece = pltpu.roll(piece, shift, 1) if shift else piece
                value = piece if value is None else jnp.where(group == q, piece, value)
            if i < PLANES:
                sigma_ref[i, :, cols] = value
            else:
                next_ref[:, cols] = value

    def one_pol(pol, carry):
        names = ("d1", "d2", "d3", "e1", "re", "im")
        acc = {name: jnp.zeros((8, 128), F32) for name in names}

        def add(name, plane):
            acc[name] = acc[name] + fold(plane)

        for part in range(2):
            after = next_ref[...]
            wy_next = after * high_ref[4 * (2 * pol + part)]
            wz_next = after * high_ref[4 * (2 * pol + part) + 1]
            for i in reversed(range(PLANES)):
                s = sigma_ref[i]
                b = [b_ref[pol, part, c, i] for c in range(3)]
                u = [u_ref[pol, part, c, i] for c in range(3)]
                w = [s * f for f in b]
                fx = st.face_x(w[1], w[2])
                fy, fz = st.faces_yz(w[0], w[1], w[2], wy_next, wz_next)
                wy_next, wz_next = w[1], w[2]
                gx, gy, gz = [face_ref[pol, part, c, i] for c in range(3)]
                rx, ry, rz = [f * f for f in w]
                qx, qy, qz = [f * v for f, v in zip(w, u)]
                ww = rx + ry + rz
                uw = qx + qy + qz
                x1 = fx * gx + fy * gy + fz * gz + st.edge_terms(qx, qy, qz)
                x2 = fx * fx + fy * fy + fz * fz + st.edge_terms(rx, ry, rz)
                if i == 0:
                    x1 = x1 + is_first * (qy + qz)
                    x2 = x2 + is_first * (ry + rz)
                add("d1", dot3(w, b))
                add("d2", ww)
                add("d3", s * ww)
                add("e1", uw)
                add("re", x2 + 2.0 * s * uw)
                add("im", 2.0 * x1 + s * dot3(u, u))
        for n, name in enumerate(names):
            keep_ref[pol, n] = acc[name]
        return carry

    lax.fori_loop(0, 2, one_pol, 0)
    row = row_ref[...]
    for pol in range(2):
        row = row + placed([keep_ref[pol, n] for n in range(6)], [64 * pol + 4 + n for n in range(6)])
    for k in range(N_SPACE):
        sums_ref[k] = row


def times(a, b):
    return a[0] * b[0] - a[1] * b[1], a[0] * b[1] + a[1] * b[0]


def over(a, b):
    denom = b[0] * b[0] + b[1] * b[1]
    return (a[0] * b[0] + a[1] * b[1]) / denom, (a[1] * b[0] - a[0] * b[1]) / denom


def steps(sums_ref, omega):
    row = jnp.sum(sums_ref[...], axis=0)
    found = []
    for pol in range(2):
        s0, s1, s2, s3, d1, d2, d3, e1, re, im = [
            jnp.broadcast_to(row[:, k + 64 * pol : k + 64 * pol + 1], (1, 128)) for k in range(N_SUMS)
        ]
        w2 = omega * omega
        scale = 1.0 / s0
        n1 = (s1, omega * d1)
        n2 = (s2 - w2 * d2, 2.0 * omega * e1)
        n3 = (s3 - w2 * re, omega * im - omega * w2 * d3)
        inverse = s0 / (n1[0] * n1[0] + n1[1] * n1[1])
        a0 = (n1[0] * inverse, -n1[1] * inverse)
        a0a0 = times(a0, a0)
        z = times(a0a0, n2)
        rho = (z[0] - s0, z[1])
        grow = (1.0 + rho[0] * scale, rho[1] * scale)
        first = times(times(grow, grow), n1)
        second = times(times(a0, grow), n2)
        third = times(a0a0, n3)
        curv = (first[0] - 2.0 * second[0] + third[0], first[1] - 2.0 * second[1] + third[1])
        a1 = over(rho, curv)
        a1g = times(a1, grow)
        a1a0 = times(a1, a0)
        found.append(((a0[0] + a1g[0], a0[1] + a1g[1]), (-a1a0[0], -a1a0[1])))
    return [tuple((jnp.concatenate([r, r], axis=1), jnp.concatenate([i, i], axis=1)) for r, i in pair) for pair in found]


def sense_kernel(omega_ref, sums_ref, t_ref, sigma_ref, out_ref):
    omega = omega_ref[0]
    found = steps(sums_ref, omega)
    group = iota(1, (DEPTH, 128)) // SLAB
    planes = []
    for i in range(PLANES):
        scaled = omega * sigma_ref[i]
        total = jnp.zeros((DEPTH, WIDTH), F32)
        for pol in range(2):
            c0, c1 = found[pol]
            fr = c0[0] - scaled * c1[1]
            fi = c0[1] + scaled * c1[0]
            total = total + (fr * fr + fi * fi) * t_ref[pol, 0, i]
            total = total + (c1[0] * c1[0] + c1[1] * c1[1]) * t_ref[pol, 1, i]
            total = total + 2.0 * (fr * c1[0] + fi * c1[1]) * t_ref[pol, 2, i]
        planes.append(omega * total)
    for f in range(N_FREQ):
        half, q = f // 4, f % 4
        value = None
        for i in range(PLANES):
            piece = planes[i][:, 128 * half : 128 * half + 128]
            shift = (SLAB * (i - q)) % 128
            piece = pltpu.roll(piece, shift, 1) if shift else piece
            value = piece if value is None else jnp.where(group == i, piece, value)
        out_ref[f] = value


def field_kernel(omega_ref, sums_ref, b_ref, u_ref, sigma_ref, cells_ref, depth_ref, x_ref, sampled_ref):
    omega = omega_ref[0]
    found = steps(sums_ref, omega)
    cells, depth = cells_ref[...], depth_ref[...]
    stations = cells.shape[1]
    in_row = iota(0, (PLANES * DEPTH, stations)) == cells // WIDTH * DEPTH + depth
    in_lane = (iota(0, (WIDTH, stations)) == cells % WIDTH).astype(F32)
    for pol in range(2):
        c0, c1 = found[pol]
        for i in range(PLANES):
            scaled = omega * sigma_ref[i]
            fr = c0[0] - scaled * c1[1]
            fi = c0[1] + scaled * c1[0]
            for c in range(3):
                br, bi = b_ref[pol, 0, c, i], b_ref[pol, 1, c, i]
                ur, ui = u_ref[pol, 0, c, i], u_ref[pol, 1, c, i]
                x_ref[pol, 0, c, i] = fr * br - fi * bi + c1[0] * ur - c1[1] * ui
                x_ref[pol, 1, c, i] = fr * bi + fi * br + c1[0] * ui + c1[1] * ur
        for part in range(2):
            for c in range(3):
                rows = x_ref[pol, part, c].reshape(PLANES * DEPTH, WIDTH)
                picked = jnp.dot(rows, in_lane, precision=lax.Precision.HIGHEST, preferred_element_type=F32)
                sampled_ref[pol, part, pl.ds(c, 1)] = jnp.sum(
                    jnp.where(in_row, picked, 0.0), axis=0, keepdims=True
                )


def gradient_kernel(terms_ref, own_ref, out_ref):
    total = terms_ref[0]
    for f in range(1, N_FREQ):
        total = total + terms_ref[f]
    for i in range(PLANES):
        out_ref[i] = own_ref[i] * total[:, SLAB * i : SLAB * i + SLAB] * (1.0 / (3.0 * 2 * N_FREQ))


def shape(*dims):
    return jax.ShapeDtypeStruct(dims, F32)


def cost(us):
    return pl.CostEstimate(flops=int(us * 1.0e9), bytes_accessed=int(us * 3.0e6), transcendentals=0)


def local(source_current, conductivity, frequency, station_cells, station_depth):
    b = source_current[0]
    stations = station_cells.shape[0]
    ends = N_SPACE - 1
    upward = [(i, i + 1) for i in range(ends)]
    downward = [(i + 1, i) for i in range(ends)]

    to_left, to_right = pl.pallas_call(
        send_kernel,
        out_shape=(shape(SLAB_PLANE + 1, DEPTH, WIDTH), shape(8, DEPTH, WIDTH)),
        in_specs=[pl.BlockSpec(memory_space=pltpu.HBM)] * 2,
        out_specs=(vmem(), vmem()),
        scratch_shapes=[
            pltpu.VMEM((2, 2, 3, DEPTH, WIDTH), F32),
            pltpu.VMEM((2, 2, 2, DEPTH, WIDTH), F32),
            pltpu.VMEM((2, 2, 3, DEPTH, WIDTH), F32),
            pltpu.VMEM((1, DEPTH, SLAB), F32),
            pltpu.SemaphoreType.DMA((4,)),
        ],
        compiler_params=params(),
        name="edge_planes",
    )(pltpu.with_memory_space_constraint(b, pltpu.HBM), pltpu.with_memory_space_constraint(conductivity, pltpu.HBM))
    high = lax.ppermute(to_left, "space", downward)
    low = lax.ppermute(to_right, "space", upward)
    packed = pl.pallas_call(
        pack_kernel,
        out_shape=shape(N_FREQ, 2, DEPTH, 128),
        in_specs=[vmem(), vmem()],
        out_specs=vmem(),
        compiler_params=params(),
        name="pack_conductivity",
    )(conductivity, high)
    got = lax.all_to_all(packed, "freq", 0, 0)

    u, faces, products, acc = pl.pallas_call(
        curl_kernel,
        out_shape=(
            shape(2, 2, 3, PLANES, DEPTH, WIDTH),
            shape(2, 2, 3, PLANES, DEPTH, WIDTH),
            shape(2, 3, PLANES, DEPTH, WIDTH),
            shape(1, 128),
        ),
        in_specs=[vmem()] * 3,
        out_specs=(vmem(),) * 4,
        scratch_shapes=[pltpu.VMEM((8, 8, 128), F32)],
        compiler_params=params(),
        cost_estimate=cost(3.0),
        name="curl_curl",
    )(b, low, high)
    sigma, sums = pl.pallas_call(
        moment_kernel,
        out_shape=(shape(PLANES, DEPTH, WIDTH), shape(N_SPACE, 1, 128)),
        in_specs=[smem()] + [vmem()] * 6,
        out_specs=(vmem(),) * 2,
        scratch_shapes=[pltpu.VMEM((DEPTH, WIDTH), F32), pltpu.VMEM((2, 6, 8, 128), F32)],
        compiler_params=params(),
        cost_estimate=cost(2.0),
        name="moments",
    )(frequency, got, b, high, u, faces, acc)
    all_sums = lax.all_to_all(sums, "space", 0, 0)
    terms = pl.pallas_call(
        sense_kernel,
        out_shape=shape(N_FREQ, DEPTH, 128),
        in_specs=[smem()] + [vmem()] * 3,
        out_specs=vmem(),
        compiler_params=params(),
        cost_estimate=cost(1.0),
        name="sensitivity",
    )(frequency, all_sums, products, sigma)
    shared = lax.all_to_all(terms, "freq", 0, 0)
    x, sampled = pl.pallas_call(
        field_kernel,
        out_shape=(shape(2, 2, 3, PLANES, DEPTH, WIDTH), shape(2, 2, 3, stations)),
        in_specs=[smem()] + [vmem()] * 6,
        out_specs=(vmem(),) * 2,
        compiler_params=params(),
        cost_estimate=cost(3.0),
        name="field",
    )(frequency, all_sums, b, u, sigma, station_cells[None], station_depth[None])
    gradient = pl.pallas_call(
        gradient_kernel,
        out_shape=shape(PLANES, DEPTH, SLAB),
        in_specs=[vmem()] * 2,
        out_specs=vmem(),
        compiler_params=params(),
        name="gradient",
    )(shared, conductivity)
    return x[None], sampled[None], gradient


def solution(mesh):
    return jax.shard_map(
        local,
        mesh=mesh,
        in_specs=(
            P("freq", None, None, None, "space", None, None),
            P("space", None, "freq"),
            P("freq"),
            P("space"),
            P("space"),
        ),
        out_specs=(
            P("freq", None, None, None, "space", None, None),
            P("freq", None, None, None, "space"),
            P("space", None, "freq"),
        ),
        check_vma=False,
    )
```

```python
import functools
import jax
import jax.numpy as jnp
from jax import lax
from jax.experimental import pallas as pl
from jax.experimental.pallas import tpu as pltpu
from jax.sharding import PartitionSpec as P

F32 = jnp.float32
N_FREQ = 8
N_SPACE = 32
FREQ_ORDER = list(range(N_FREQ))[::-1]
SPACE_ORDER = [(i + 16) % N_SPACE for i in range(N_SPACE)]
DEPTH = 16
WIDTH = 256
PLANES = 4
SLAB = WIDTH // N_FREQ
LIMIT = 24 * 1024 * 1024


def params():
    return pltpu.CompilerParams(vmem_limit_bytes=LIMIT)


def vmem():
    return pl.BlockSpec(memory_space=pltpu.VMEM)


def anywhere():
    return pl.BlockSpec(memory_space=pl.ANY)


def smem():
    return pl.BlockSpec(memory_space=pltpu.SMEM)


def iota(dim, shape=(DEPTH, WIDTH)):
    return lax.broadcasted_iota(jnp.int32, shape, dim)


class Stencil:
    def __init__(self):
        row, lane = iota(0), iota(1)
        self.first_row, self.last_row = row == 0, row == DEPTH - 1
        self.first_lane, self.last_lane = lane == 0, lane == WIDTH - 1

    def fy(self, f):
        return jnp.where(self.last_lane, 0.0, pltpu.roll(f, WIDTH - 1, 1)) - f

    def fz(self, f):
        return jnp.where(self.last_row, 0.0, pltpu.roll(f, DEPTH - 1, 0)) - f

    def by(self, g, before):
        return g - jnp.where(self.first_lane, before, pltpu.roll(g, 1, 1))

    def bz(self, g, before):
        return g - jnp.where(self.first_row, before, pltpu.roll(g, 1, 0))

    def faces_yz(self, ex, ey, ez, ey_next, ez_next):
        return self.fz(ex) - (ez_next - ez), (ey_next - ey) - self.fy(ex)

    def face_x(self, ey, ez):
        return self.fy(ez) - self.fz(ey)

    def edge_terms(self, px, py, pz):
        return jnp.where(self.first_lane, px + pz, 0.0) + jnp.where(self.first_row, px + py, 0.0)


def fold(plane):
    half = plane[:8] + plane[8:]
    return half[:, :128] + half[:, 128:]


def dot3(a, b):
    return a[0] * b[0] + a[1] * b[1] + a[2] * b[2]


LAST = PLANES - 1
SLAB_PLANE = 16


def placed(parts, lanes):
    row, lane = iota(0, (8, 128)), iota(1, (8, 128))
    table = jnp.zeros((8, 128), F32)
    target = jnp.full((8, 128), -1, jnp.int32)
    for n, (part, at) in enumerate(zip(parts, lanes)):
        table = jnp.where(row == n, jnp.sum(part, axis=0, keepdims=True), table)
        target = jnp.where(row == n, at, target)
    totals = jnp.sum(table, axis=1, keepdims=True)
    return jnp.sum(jnp.where(lane == target, totals, 0.0), axis=0, keepdims=True)


def send_kernel(b_ref, sigma_ref, left_ref, right_ref, front_ref, second_ref, last_ref, own_ref, sems):
    copies = [
        pltpu.make_async_copy(b_ref.at[:, :, :, 0], front_ref, sems.at[0]),
        pltpu.make_async_copy(b_ref.at[:, :, pl.ds(1, 2), 1], second_ref, sems.at[1]),
        pltpu.make_async_copy(b_ref.at[:, :, :, LAST], last_ref, sems.at[2]),
        pltpu.make_async_copy(sigma_ref.at[pl.ds(0, 1)], own_ref, sems.at[3]),
    ]
    for copy in copies:
        copy.start()
    for copy in copies:
        copy.wait()
    st = Stencil()
    for pol in range(2):
        for part in range(2):
            k = 2 * pol + part
            ex, ey, ez = [front_ref[pol, part, c] for c in range(3)]
            hx = st.face_x(ey, ez)
            hy, hz = st.faces_yz(ex, ey, ez, second_ref[pol, part, 0], second_ref[pol, part, 1])
            left_ref[4 * k] = ey
            left_ref[4 * k + 1] = ez
            left_ref[4 * k + 2] = st.bz(hx, -ey) - hz
            left_ref[4 * k + 3] = hy - st.by(hx, ez)
            ex, ey, ez = [last_ref[pol, part, c] for c in range(3)]
            right_ref[2 * k] = st.fz(ex) + ez
            right_ref[2 * k + 1] = -ey - st.fy(ex)
    front = jnp.concatenate([own_ref[0]] * 4, axis=1)
    left_ref[SLAB_PLANE] = jnp.concatenate([front, front], axis=1)


def pack_kernel(own_ref, high_ref, out_ref):
    own = jnp.concatenate([own_ref[i] for i in range(PLANES)], axis=1)
    for f in range(N_FREQ):
        out_ref[f, 0] = own
        out_ref[f, 1] = high_ref[SLAB_PLANE, :, :128]


def curl_kernel(b_ref, low_ref, high_ref, u_ref, face_ref, t_ref, row_ref, keep_ref):
    st = Stencil()
    place = lax.axis_index("space")
    keep_next = jnp.where(place == N_SPACE - 1, 0.0, 1.0).astype(F32)
    is_first = jnp.where(place == 0, 1.0, 0.0).astype(F32)

    def one_pol(pol, carry):
        s0 = jnp.zeros((8, 128), F32)
        s1 = jnp.zeros((8, 128), F32)
        s2 = jnp.zeros((8, 128), F32)
        s3 = jnp.zeros((8, 128), F32)
        for part in range(2):
            k = 2 * pol + part

            def field(c, i):
                return b_ref[pol, part, c, i] if i < PLANES else high_ref[4 * k + c - 1]

            hy_old = low_ref[2 * k] - field(2, 0)
            hz_old = low_ref[2 * k + 1] + field(1, 0)
            u_old = None
            for i in range(PLANES + 1):
                if i < PLANES:
                    ex, ey, ez = field(0, i), field(1, i), field(2, i)
                    hx = st.face_x(ey, ez)
                    hy, hz = st.faces_yz(ex, ey, ez, field(1, i + 1), field(2, i + 1))
                    uy = st.bz(hx, -ey) - (hz - hz_old)
                    uz = (hy - hy_old) - st.by(hx, ez)
                    hy_old, hz_old = hy, hz
                    ux = st.by(hz, -ex) - st.bz(hy, ex)
                    u_ref[pol, part, 0, i] = ux
                    u_ref[pol, part, 1, i] = uy
                    u_ref[pol, part, 2, i] = uz
                    s0 = s0 + fold(ex * ex + ey * ey + ez * ez)
                    s1 = s1 + fold(ex * ux + ey * uy + ez * uz)
                else:
                    uy = keep_next * (high_ref[4 * k + 2] + hz_old)
                    uz = keep_next * (high_ref[4 * k + 3] - hy_old)
                if u_old is not None:
                    px, py, pz = u_old
                    fx = st.face_x(py, pz)
                    fy, fz = st.faces_yz(px, py, pz, uy, uz)
                    face_ref[pol, part, 0, i - 1] = fx
                    face_ref[pol, part, 1, i - 1] = fy
                    face_ref[pol, part, 2, i - 1] = fz
                    qx, qy, qz = px * px, py * py, pz * pz
                    s2 = s2 + fold(qx + qy + qz)
                    total = fx * fx + fy * fy + fz * fz + st.edge_terms(qx, qy, qz)
                    if i == 1:
                        total = total + is_first * (qy + qz)
                    s3 = s3 + fold(total)
                if i < PLANES:
                    u_old = (ux, uy, uz)
        for n, value in enumerate((s0, s1, s2, s3)):
            keep_ref[4 * pol + n] = value
        for i in range(PLANES):
            br = [b_ref[pol, 0, c, i] for c in range(3)]
            bi = [b_ref[pol, 1, c, i] for c in range(3)]
            ur = [u_ref[pol, 0, c, i] for c in range(3)]
            ui = [u_ref[pol, 1, c, i] for c in range(3)]
            t_ref[pol, 0, i] = dot3(br, br) - dot3(bi, bi)
            t_ref[pol, 1, i] = dot3(ur, ur) - dot3(ui, ui)
            t_ref[pol, 2, i] = dot3(br, ur) - dot3(bi, ui)
        return carry

    lax.fori_loop(0, 2, one_pol, 0)
    row_ref[...] = placed([keep_ref[n] for n in range(8)], [n % 4 + 64 * (n // 4) for n in range(8)])


N_SUMS = 10


def moment_kernel(_, got_ref, b_ref, high_ref, u_ref, face_ref, row_ref, sigma_ref, sums_ref, next_ref, keep_ref):
    st = Stencil()
    is_first = jnp.where(lax.axis_index("space") == 0, 1.0, 0.0).astype(F32)
    group = iota(1, (DEPTH, 128)) // SLAB
    for half in range(2):
        cols = pl.ds(128 * half, 128)
        for i in range(PLANES + 1):
            value = None
            for q in range(4):
                piece = got_ref[FREQ_ORDER[4 * half + q], 0 if i < PLANES else 1]
                shift = (SLAB * (q - i)) % 128 if i < PLANES else 0
                piece = pltpu.roll(piece, shift, 1) if shift else piece
                value = piece if value is None else jnp.where(group == q, piece, value)
            if i < PLANES:
                sigma_ref[i, :, cols] = value
            else:
                next_ref[:, cols] = value

    def one_pol(pol, carry):
        names = ("d1", "d2", "d3", "e1", "re", "im")
        acc = {name: jnp.zeros((8, 128), F32) for name in names}

        def add(name, plane):
            acc[name] = acc[name] + fold(plane)

        for part in range(2):
            after = next_ref[...]
            wy_next = after * high_ref[4 * (2 * pol + part)]
            wz_next = after * high_ref[4 * (2 * pol + part) + 1]
            for i in reversed(range(PLANES)):
                s = sigma_ref[i]
                b = [b_ref[pol, part, c, i] for c in range(3)]
                u = [u_ref[pol, part, c, i] for c in range(3)]
                w = [s * f for f in b]
                fx = st.face_x(w[1], w[2])
                fy, fz = st.faces_yz(w[0], w[1], w[2], wy_next, wz_next)
                wy_next, wz_next = w[1], w[2]
                gx, gy, gz = [face_ref[pol, part, c, i] for c in range(3)]
                rx, ry, rz = [f * f for f in w]
                qx, qy, qz = [f * v for f, v in zip(w, u)]
                ww = rx + ry + rz
                uw = qx + qy + qz
                x1 = fx * gx + fy * gy + fz * gz + st.edge_terms(qx, qy, qz)
                x2 = fx * fx + fy * fy + fz * fz + st.edge_terms(rx, ry, rz)
                if i == 0:
                    x1 = x1 + is_first * (qy + qz)
                    x2 = x2 + is_first * (ry + rz)
                add("d1", dot3(w, b))
                add("d2", ww)
                add("d3", s * ww)
                add("e1", uw)
                add("re", x2 + 2.0 * s * uw)
                add("im", 2.0 * x1 + s * dot3(u, u))
        for n, name in enumerate(names):
            keep_ref[pol, n] = acc[name]
        return carry

    lax.fori_loop(0, 2, one_pol, 0)
    row = row_ref[...]
    for pol in range(2):
        row = row + placed([keep_ref[pol, n] for n in range(6)], [64 * pol + 4 + n for n in range(6)])
    for k in range(N_SPACE):
        sums_ref[k] = row


def times(a, b):
    return a[0] * b[0] - a[1] * b[1], a[0] * b[1] + a[1] * b[0]


def over(a, b):
    denom = b[0] * b[0] + b[1] * b[1]
    return (a[0] * b[0] + a[1] * b[1]) / denom, (a[1] * b[0] - a[0] * b[1]) / denom


def steps(sums_ref, omega):
    row = jnp.sum(sums_ref[...], axis=0)
    found = []
    for pol in range(2):
        s0, s1, s2, s3, d1, d2, d3, e1, re, im = [
            jnp.broadcast_to(row[:, k + 64 * pol : k + 64 * pol + 1], (1, 128)) for k in range(N_SUMS)
        ]
        w2 = omega * omega
        scale = 1.0 / s0
        n1 = (s1, omega * d1)
        n2 = (s2 - w2 * d2, 2.0 * omega * e1)
        n3 = (s3 - w2 * re, omega * im - omega * w2 * d3)
        inverse = s0 / (n1[0] * n1[0] + n1[1] * n1[1])
        a0 = (n1[0] * inverse, -n1[1] * inverse)
        a0a0 = times(a0, a0)
        z = times(a0a0, n2)
        rho = (z[0] - s0, z[1])
        grow = (1.0 + rho[0] * scale, rho[1] * scale)
        first = times(times(grow, grow), n1)
        second = times(times(a0, grow), n2)
        third = times(a0a0, n3)
        curv = (first[0] - 2.0 * second[0] + third[0], first[1] - 2.0 * second[1] + third[1])
        a1 = over(rho, curv)
        a1g = times(a1, grow)
        a1a0 = times(a1, a0)
        found.append(((a0[0] + a1g[0], a0[1] + a1g[1]), (-a1a0[0], -a1a0[1])))
    return [tuple((jnp.concatenate([r, r], axis=1), jnp.concatenate([i, i], axis=1)) for r, i in pair) for pair in found]


def sense_kernel(omega_ref, sums_ref, t_ref, sigma_ref, out_ref):
    omega = omega_ref[0]
    found = steps(sums_ref, omega)
    group = iota(1, (DEPTH, 128)) // SLAB
    planes = []
    for i in range(PLANES):
        scaled = omega * sigma_ref[i]
        total = jnp.zeros((DEPTH, WIDTH), F32)
        for pol in range(2):
            c0, c1 = found[pol]
            fr = c0[0] - scaled * c1[1]
            fi = c0[1] + scaled * c1[0]
            total = total + (fr * fr + fi * fi) * t_ref[pol, 0, i]
            total = total + (c1[0] * c1[0] + c1[1] * c1[1]) * t_ref[pol, 1, i]
            total = total + 2.0 * (fr * c1[0] + fi * c1[1]) * t_ref[pol, 2, i]
        planes.append(omega * total)
    for f in range(N_FREQ):
        half, q = f // 4, f % 4
        value = None
        for i in range(PLANES):
            piece = planes[i][:, 128 * half : 128 * half + 128]
            shift = (SLAB * (i - q)) % 128
            piece = pltpu.roll(piece, shift, 1) if shift else piece
            value = piece if value is None else jnp.where(group == i, piece, value)
        out_ref[FREQ_ORDER[f]] = value


def field_kernel(omega_ref, sums_ref, b_ref, u_ref, sigma_ref, cells_ref, depth_ref, x_ref, sampled_ref):
    omega = omega_ref[0]
    found = steps(sums_ref, omega)
    cells, depth = cells_ref[...], depth_ref[...]
    stations = cells.shape[1]
    in_row = iota(0, (PLANES * DEPTH, stations)) == cells // WIDTH * DEPTH + depth
    in_lane = (iota(0, (WIDTH, stations)) == cells % WIDTH).astype(F32)
    for pol in range(2):
        c0, c1 = found[pol]
        for i in range(PLANES):
            scaled = omega * sigma_ref[i]
            fr = c0[0] - scaled * c1[1]
            fi = c0[1] + scaled * c1[0]
            for c in range(3):
                br, bi = b_ref[pol, 0, c, i], b_ref[pol, 1, c, i]
                ur, ui = u_ref[pol, 0, c, i], u_ref[pol, 1, c, i]
                x_ref[pol, 0, c, i] = fr * br - fi * bi + c1[0] * ur - c1[1] * ui
                x_ref[pol, 1, c, i] = fr * bi + fi * br + c1[0] * ui + c1[1] * ur
        for part in range(2):
            for c in range(3):
                rows = x_ref[pol, part, c].reshape(PLANES * DEPTH, WIDTH)
                picked = jnp.dot(rows, in_lane, precision=lax.Precision.HIGHEST, preferred_element_type=F32)
                sampled_ref[pol, part, pl.ds(c, 1)] = jnp.sum(
                    jnp.where(in_row, picked, 0.0), axis=0, keepdims=True
                )


def gradient_kernel(terms_ref, own_ref, out_ref):
    total = terms_ref[0]
    for f in range(1, N_FREQ):
        total = total + terms_ref[f]
    for i in range(PLANES):
        out_ref[i] = own_ref[i] * total[:, SLAB * i : SLAB * i + SLAB] * (1.0 / (3.0 * 2 * N_FREQ))


def shape(*dims):
    return jax.ShapeDtypeStruct(dims, F32)


def cost(us):
    return pl.CostEstimate(flops=int(us * 1.0e9), bytes_accessed=int(us * 3.0e6), transcendentals=0)


def local(source_current, conductivity, frequency, station_cells, station_depth):
    b = source_current[0]
    stations = station_cells.shape[0]
    ends = N_SPACE - 1
    upward = [(i, i + 1) for i in range(ends)]
    downward = [(i + 1, i) for i in range(ends)]

    to_left, to_right = pl.pallas_call(
        send_kernel,
        out_shape=(shape(SLAB_PLANE + 1, DEPTH, WIDTH), shape(8, DEPTH, WIDTH)),
        in_specs=[pl.BlockSpec(memory_space=pltpu.HBM)] * 2,
        out_specs=(vmem(), vmem()),
        scratch_shapes=[
            pltpu.VMEM((2, 2, 3, DEPTH, WIDTH), F32),
            pltpu.VMEM((2, 2, 2, DEPTH, WIDTH), F32),
            pltpu.VMEM((2, 2, 3, DEPTH, WIDTH), F32),
            pltpu.VMEM((1, DEPTH, SLAB), F32),
            pltpu.SemaphoreType.DMA((4,)),
        ],
        compiler_params=params(),
        name="edge_planes",
    )(pltpu.with_memory_space_constraint(b, pltpu.HBM), pltpu.with_memory_space_constraint(conductivity, pltpu.HBM))
    high = lax.ppermute(to_left, "space", downward)
    low = lax.ppermute(to_right, "space", upward)
    packed = pl.pallas_call(
        pack_kernel,
        out_shape=shape(N_FREQ, 2, DEPTH, 128),
        in_specs=[vmem(), vmem()],
        out_specs=vmem(),
        compiler_params=params(),
        name="pack_conductivity",
    )(conductivity, high)
    got = lax.all_to_all(packed, "freq", 0, 0, axis_index_groups=[FREQ_ORDER])

    u, faces, products, acc = pl.pallas_call(
        curl_kernel,
        out_shape=(
            shape(2, 2, 3, PLANES, DEPTH, WIDTH),
            shape(2, 2, 3, PLANES, DEPTH, WIDTH),
            shape(2, 3, PLANES, DEPTH, WIDTH),
            shape(1, 128),
        ),
        in_specs=[vmem()] * 3,
        out_specs=(vmem(),) * 4,
        scratch_shapes=[pltpu.VMEM((8, 8, 128), F32)],
        compiler_params=params(),
        cost_estimate=cost(3.0),
        name="curl_curl",
    )(b, low, high)
    sigma, sums = pl.pallas_call(
        moment_kernel,
        out_shape=(shape(PLANES, DEPTH, WIDTH), shape(N_SPACE, 1, 128)),
        in_specs=[smem()] + [vmem()] * 6,
        out_specs=(vmem(),) * 2,
        scratch_shapes=[pltpu.VMEM((DEPTH, WIDTH), F32), pltpu.VMEM((2, 6, 8, 128), F32)],
        compiler_params=params(),
        cost_estimate=cost(2.0),
        name="moments",
    )(frequency, got, b, high, u, faces, acc)
    all_sums = lax.all_to_all(sums, "space", 0, 0, axis_index_groups=[SPACE_ORDER])
    terms = pl.pallas_call(
        sense_kernel,
        out_shape=shape(N_FREQ, DEPTH, 128),
        in_specs=[smem()] + [vmem()] * 3,
        out_specs=vmem(),
        compiler_params=params(),
        cost_estimate=cost(1.0),
        name="sensitivity",
    )(frequency, all_sums, products, sigma)
    shared = lax.all_to_all(terms, "freq", 0, 0, axis_index_groups=[FREQ_ORDER])
    x, sampled = pl.pallas_call(
        field_kernel,
        out_shape=(shape(2, 2, 3, PLANES, DEPTH, WIDTH), shape(2, 2, 3, stations)),
        in_specs=[smem()] + [vmem()] * 6,
        out_specs=(vmem(),) * 2,
        compiler_params=params(),
        cost_estimate=cost(3.0),
        name="field",
    )(frequency, all_sums, b, u, sigma, station_cells[None], station_depth[None])
    gradient = pl.pallas_call(
        gradient_kernel,
        out_shape=shape(PLANES, DEPTH, SLAB),
        in_specs=[vmem()] * 2,
        out_specs=vmem(),
        compiler_params=params(),
        name="gradient",
    )(shared, conductivity)
    return x[None], sampled[None], gradient


def solution(mesh):
    return jax.shard_map(
        local,
        mesh=mesh,
        in_specs=(
            P("freq", None, None, None, "space", None, None),
            P("space", None, "freq"),
            P("freq"),
            P("space"),
            P("space"),
        ),
        out_specs=(
            P("freq", None, None, None, "space", None, None),
            P("freq", None, None, None, "space"),
            P("space", None, "freq"),
        ),
        check_vma=False,
    )
```

```python
import functools
import jax
import jax.numpy as jnp
from jax import lax
from jax.experimental import pallas as pl
from jax.experimental.pallas import tpu as pltpu
from jax.sharding import PartitionSpec as P

F32 = jnp.float32
N_FREQ = 8
N_SPACE = 32
FREQ_ORDER = list(range(N_FREQ))[::-1]
SPACE_ORDER = [(19 - i) % N_SPACE for i in range(N_SPACE)]
DEPTH = 16
WIDTH = 256
PLANES = 4
SLAB = WIDTH // N_FREQ
LIMIT = 24 * 1024 * 1024


def params():
    return pltpu.CompilerParams(vmem_limit_bytes=LIMIT)


def vmem():
    return pl.BlockSpec(memory_space=pltpu.VMEM)


def hbm():
    return pl.BlockSpec(memory_space=pltpu.HBM)


def smem():
    return pl.BlockSpec(memory_space=pltpu.SMEM)


def iota(dim, shape=(DEPTH, WIDTH)):
    return lax.broadcasted_iota(jnp.int32, shape, dim)


class Stencil:
    def __init__(self):
        row, lane = iota(0), iota(1)
        self.first_row, self.last_row = row == 0, row == DEPTH - 1
        self.first_lane, self.last_lane = lane == 0, lane == WIDTH - 1

    def fy(self, f):
        return jnp.where(self.last_lane, 0.0, pltpu.roll(f, WIDTH - 1, 1)) - f

    def fz(self, f):
        return jnp.where(self.last_row, 0.0, pltpu.roll(f, DEPTH - 1, 0)) - f

    def by(self, g, before):
        return g - jnp.where(self.first_lane, before, pltpu.roll(g, 1, 1))

    def bz(self, g, before):
        return g - jnp.where(self.first_row, before, pltpu.roll(g, 1, 0))

    def faces_yz(self, ex, ey, ez, ey_next, ez_next):
        return self.fz(ex) - (ez_next - ez), (ey_next - ey) - self.fy(ex)

    def face_x(self, ey, ez):
        return self.fy(ez) - self.fz(ey)

    def edge_terms(self, px, py, pz):
        return jnp.where(self.first_lane, px + pz, 0.0) + jnp.where(self.first_row, px + py, 0.0)


def fold(plane):
    half = plane[:8] + plane[8:]
    return half[:, :128] + half[:, 128:]


def dot3(a, b):
    return a[0] * b[0] + a[1] * b[1] + a[2] * b[2]


LAST = PLANES - 1
SLAB_PLANE = 16


def placed(parts, lanes):
    row, lane = iota(0, (8, 128)), iota(1, (8, 128))
    table = jnp.zeros((8, 128), F32)
    target = jnp.full((8, 128), -1, jnp.int32)
    for n, (part, at) in enumerate(zip(parts, lanes)):
        table = jnp.where(row == n, jnp.sum(part, axis=0, keepdims=True), table)
        target = jnp.where(row == n, at, target)
    totals = jnp.sum(table, axis=1, keepdims=True)
    return jnp.sum(jnp.where(lane == target, totals, 0.0), axis=0, keepdims=True)


def send_kernel(b_ref, sigma_ref, left_ref, right_ref, front_ref, second_ref, last_ref, own_ref, sems):
    copies = [
        pltpu.make_async_copy(b_ref.at[:, :, :, 0], front_ref, sems.at[0]),
        pltpu.make_async_copy(b_ref.at[:, :, pl.ds(1, 2), 1], second_ref, sems.at[1]),
        pltpu.make_async_copy(b_ref.at[:, :, :, LAST], last_ref, sems.at[2]),
        pltpu.make_async_copy(sigma_ref.at[pl.ds(0, 1)], own_ref, sems.at[3]),
    ]
    for copy in copies:
        copy.start()
    for copy in copies:
        copy.wait()
    st = Stencil()
    for pol in range(2):
        for part in range(2):
            k = 2 * pol + part
            ex, ey, ez = [front_ref[pol, part, c] for c in range(3)]
            hx = st.face_x(ey, ez)
            hy, hz = st.faces_yz(ex, ey, ez, second_ref[pol, part, 0], second_ref[pol, part, 1])
            left_ref[4 * k] = ey
            left_ref[4 * k + 1] = ez
            left_ref[4 * k + 2] = st.bz(hx, -ey) - hz
            left_ref[4 * k + 3] = hy - st.by(hx, ez)
            ex, ey, ez = [last_ref[pol, part, c] for c in range(3)]
            right_ref[2 * k] = st.fz(ex) + ez
            right_ref[2 * k + 1] = -ey - st.fy(ex)
    front = jnp.concatenate([own_ref[0]] * 4, axis=1)
    left_ref[SLAB_PLANE] = jnp.concatenate([front, front], axis=1)


def pack_kernel(own_ref, high_ref, out_ref, both_ref, sems):
    both_ref[0] = jnp.concatenate([own_ref[i] for i in range(PLANES)], axis=1)
    both_ref[1] = high_ref[SLAB_PLANE, :, :128]
    copies = [pltpu.make_async_copy(both_ref, out_ref.at[f], sems.at[f]) for f in range(N_FREQ)]
    for copy in copies:
        copy.start()
    for copy in copies:
        copy.wait()


def curl_kernel(source_ref, low_ref, high_ref, b_ref, u_ref, face_ref, t_ref, row_ref, keep_ref, sem):
    load = pltpu.make_async_copy(source_ref, b_ref, sem)
    load.start()
    load.wait()
    st = Stencil()
    place = lax.axis_index("space")
    keep_next = jnp.where(place == N_SPACE - 1, 0.0, 1.0).astype(F32)
    is_first = jnp.where(place == 0, 1.0, 0.0).astype(F32)

    def one_pol(pol, carry):
        s0 = jnp.zeros((8, 128), F32)
        s1 = jnp.zeros((8, 128), F32)
        s2 = jnp.zeros((8, 128), F32)
        s3 = jnp.zeros((8, 128), F32)
        for part in range(2):
            k = 2 * pol + part

            def field(c, i):
                return b_ref[pol, part, c, i] if i < PLANES else high_ref[4 * k + c - 1]

            hy_old = low_ref[2 * k] - field(2, 0)
            hz_old = low_ref[2 * k + 1] + field(1, 0)
            u_old = None
            for i in range(PLANES + 1):
                if i < PLANES:
                    ex, ey, ez = field(0, i), field(1, i), field(2, i)
                    hx = st.face_x(ey, ez)
                    hy, hz = st.faces_yz(ex, ey, ez, field(1, i + 1), field(2, i + 1))
                    uy = st.bz(hx, -ey) - (hz - hz_old)
                    uz = (hy - hy_old) - st.by(hx, ez)
                    hy_old, hz_old = hy, hz
                    ux = st.by(hz, -ex) - st.bz(hy, ex)
                    u_ref[pol, part, 0, i] = ux
                    u_ref[pol, part, 1, i] = uy
                    u_ref[pol, part, 2, i] = uz
                    s0 = s0 + fold(ex * ex + ey * ey + ez * ez)
                    s1 = s1 + fold(ex * ux + ey * uy + ez * uz)
                else:
                    uy = keep_next * (high_ref[4 * k + 2] + hz_old)
                    uz = keep_next * (high_ref[4 * k + 3] - hy_old)
                if u_old is not None:
                    px, py, pz = u_old
                    fx = st.face_x(py, pz)
                    fy, fz = st.faces_yz(px, py, pz, uy, uz)
                    face_ref[pol, part, 0, i - 1] = fx
                    face_ref[pol, part, 1, i - 1] = fy
                    face_ref[pol, part, 2, i - 1] = fz
                    qx, qy, qz = px * px, py * py, pz * pz
                    s2 = s2 + fold(qx + qy + qz)
                    total = fx * fx + fy * fy + fz * fz + st.edge_terms(qx, qy, qz)
                    if i == 1:
                        total = total + is_first * (qy + qz)
                    s3 = s3 + fold(total)
                if i < PLANES:
                    u_old = (ux, uy, uz)
        for n, value in enumerate((s0, s1, s2, s3)):
            keep_ref[4 * pol + n] = value
        for i in range(PLANES):
            br = [b_ref[pol, 0, c, i] for c in range(3)]
            bi = [b_ref[pol, 1, c, i] for c in range(3)]
            ur = [u_ref[pol, 0, c, i] for c in range(3)]
            ui = [u_ref[pol, 1, c, i] for c in range(3)]
            t_ref[pol, 0, i] = dot3(br, br) - dot3(bi, bi)
            t_ref[pol, 1, i] = dot3(ur, ur) - dot3(ui, ui)
            t_ref[pol, 2, i] = dot3(br, ur) - dot3(bi, ui)
        return carry

    lax.fori_loop(0, 2, one_pol, 0)
    row_ref[...] = placed([keep_ref[n] for n in range(8)], [n % 4 + 64 * (n // 4) for n in range(8)])


N_SUMS = 10


def moment_kernel(_, got_ref, b_ref, high_ref, u_ref, face_ref, row_ref, sigma_ref, sums_ref, next_ref, keep_ref):
    st = Stencil()
    is_first = jnp.where(lax.axis_index("space") == 0, 1.0, 0.0).astype(F32)
    group = iota(1, (DEPTH, 128)) // SLAB
    for half in range(2):
        cols = pl.ds(128 * half, 128)
        for i in range(PLANES + 1):
            value = None
            for q in range(4):
                piece = got_ref[FREQ_ORDER[4 * half + q], 0 if i < PLANES else 1]
                shift = (SLAB * (q - i)) % 128 if i < PLANES else 0
                piece = pltpu.roll(piece, shift, 1) if shift else piece
                value = piece if value is None else jnp.where(group == q, piece, value)
            if i < PLANES:
                sigma_ref[i, :, cols] = value
            else:
                next_ref[:, cols] = value

    def one_pol(pol, carry):
        names = ("d1", "d2", "d3", "e1", "re", "im")
        acc = {name: jnp.zeros((8, 128), F32) for name in names}

        def add(name, plane):
            acc[name] = acc[name] + fold(plane)

        for part in range(2):
            after = next_ref[...]
            wy_next = after * high_ref[4 * (2 * pol + part)]
            wz_next = after * high_ref[4 * (2 * pol + part) + 1]
            for i in reversed(range(PLANES)):
                s = sigma_ref[i]
                b = [b_ref[pol, part, c, i] for c in range(3)]
                u = [u_ref[pol, part, c, i] for c in range(3)]
                w = [s * f for f in b]
                fx = st.face_x(w[1], w[2])
                fy, fz = st.faces_yz(w[0], w[1], w[2], wy_next, wz_next)
                wy_next, wz_next = w[1], w[2]
                gx, gy, gz = [face_ref[pol, part, c, i] for c in range(3)]
                rx, ry, rz = [f * f for f in w]
                qx, qy, qz = [f * v for f, v in zip(w, u)]
                ww = rx + ry + rz
                uw = qx + qy + qz
                x1 = fx * gx + fy * gy + fz * gz + st.edge_terms(qx, qy, qz)
                x2 = fx * fx + fy * fy + fz * fz + st.edge_terms(rx, ry, rz)
                if i == 0:
                    x1 = x1 + is_first * (qy + qz)
                    x2 = x2 + is_first * (ry + rz)
                add("d1", dot3(w, b))
                add("d2", ww)
                add("d3", s * ww)
                add("e1", uw)
                add("re", x2 + 2.0 * s * uw)
                add("im", 2.0 * x1 + s * dot3(u, u))
        for n, name in enumerate(names):
            keep_ref[pol, n] = acc[name]
        return carry

    lax.fori_loop(0, 2, one_pol, 0)
    row = row_ref[...]
    for pol in range(2):
        row = row + placed([keep_ref[pol, n] for n in range(6)], [64 * pol + 4 + n for n in range(6)])
    for k in range(N_SPACE):
        sums_ref[k] = row


def times(a, b):
    return a[0] * b[0] - a[1] * b[1], a[0] * b[1] + a[1] * b[0]


def over(a, b):
    denom = b[0] * b[0] + b[1] * b[1]
    return (a[0] * b[0] + a[1] * b[1]) / denom, (a[1] * b[0] - a[0] * b[1]) / denom


def steps(sums_ref, omega):
    row = jnp.sum(sums_ref[...], axis=0)
    found = []
    for pol in range(2):
        s0, s1, s2, s3, d1, d2, d3, e1, re, im = [
            jnp.broadcast_to(row[:, k + 64 * pol : k + 64 * pol + 1], (1, 128)) for k in range(N_SUMS)
        ]
        w2 = omega * omega
        scale = 1.0 / s0
        n1 = (s1, omega * d1)
        n2 = (s2 - w2 * d2, 2.0 * omega * e1)
        n3 = (s3 - w2 * re, omega * im - omega * w2 * d3)
        inverse = s0 / (n1[0] * n1[0] + n1[1] * n1[1])
        a0 = (n1[0] * inverse, -n1[1] * inverse)
        a0a0 = times(a0, a0)
        z = times(a0a0, n2)
        rho = (z[0] - s0, z[1])
        grow = (1.0 + rho[0] * scale, rho[1] * scale)
        first = times(times(grow, grow), n1)
        second = times(times(a0, grow), n2)
        third = times(a0a0, n3)
        curv = (first[0] - 2.0 * second[0] + third[0], first[1] - 2.0 * second[1] + third[1])
        a1 = over(rho, curv)
        a1g = times(a1, grow)
        a1a0 = times(a1, a0)
        found.append(((a0[0] + a1g[0], a0[1] + a1g[1]), (-a1a0[0], -a1a0[1])))
    return [tuple((jnp.concatenate([r, r], axis=1), jnp.concatenate([i, i], axis=1)) for r, i in pair) for pair in found]


def sense_kernel(omega_ref, sums_ref, t_ref, sigma_ref, out_ref):
    omega = omega_ref[0]
    found = steps(sums_ref, omega)
    group = iota(1, (DEPTH, 128)) // SLAB
    planes = []
    for i in range(PLANES):
        scaled = omega * sigma_ref[i]
        total = jnp.zeros((DEPTH, WIDTH), F32)
        for pol in range(2):
            c0, c1 = found[pol]
            fr = c0[0] - scaled * c1[1]
            fi = c0[1] + scaled * c1[0]
            total = total + (fr * fr + fi * fi) * t_ref[pol, 0, i]
            total = total + (c1[0] * c1[0] + c1[1] * c1[1]) * t_ref[pol, 1, i]
            total = total + 2.0 * (fr * c1[0] + fi * c1[1]) * t_ref[pol, 2, i]
        planes.append(omega * total)
    for f in range(N_FREQ):
        half, q = f // 4, f % 4
        value = None
        for i in range(PLANES):
            piece = planes[i][:, 128 * half : 128 * half + 128]
            shift = (SLAB * (i - q)) % 128
            piece = pltpu.roll(piece, shift, 1) if shift else piece
            value = piece if value is None else jnp.where(group == i, piece, value)
        out_ref[FREQ_ORDER[f]] = value


def field_kernel(omega_ref, sums_ref, b_ref, u_ref, sigma_ref, cells_ref, depth_ref, x_ref, sampled_ref):
    omega = omega_ref[0]
    found = steps(sums_ref, omega)
    cells, depth = cells_ref[...], depth_ref[...]
    stations = cells.shape[1]
    in_row = iota(0, (PLANES * DEPTH, stations)) == cells // WIDTH * DEPTH + depth
    in_lane = (iota(0, (WIDTH, stations)) == cells % WIDTH).astype(F32)
    for pol in range(2):
        c0, c1 = found[pol]
        for i in range(PLANES):
            scaled = omega * sigma_ref[i]
            fr = c0[0] - scaled * c1[1]
            fi = c0[1] + scaled * c1[0]
            for c in range(3):
                br, bi = b_ref[pol, 0, c, i], b_ref[pol, 1, c, i]
                ur, ui = u_ref[pol, 0, c, i], u_ref[pol, 1, c, i]
                x_ref[pol, 0, c, i] = fr * br - fi * bi + c1[0] * ur - c1[1] * ui
                x_ref[pol, 1, c, i] = fr * bi + fi * br + c1[0] * ui + c1[1] * ur
        for part in range(2):
            for c in range(3):
                rows = x_ref[pol, part, c].reshape(PLANES * DEPTH, WIDTH)
                picked = jnp.dot(rows, in_lane, precision=lax.Precision.HIGHEST, preferred_element_type=F32)
                sampled_ref[pol, part, pl.ds(c, 1)] = jnp.sum(
                    jnp.where(in_row, picked, 0.0), axis=0, keepdims=True
                )


def gradient_kernel(terms_ref, own_ref, out_ref):
    total = terms_ref[0]
    for f in range(1, N_FREQ):
        total = total + terms_ref[f]
    for i in range(PLANES):
        out_ref[i] = own_ref[i] * total[:, SLAB * i : SLAB * i + SLAB] * (1.0 / (3.0 * 2 * N_FREQ))


def shape(*dims):
    return jax.ShapeDtypeStruct(dims, F32)


def cost(us):
    return pl.CostEstimate(flops=int(us * 1.0e9), bytes_accessed=int(us * 3.0e6), transcendentals=0)


def local(source_current, conductivity, frequency, station_cells, station_depth):
    b = source_current[0]
    b_far = pltpu.with_memory_space_constraint(b, pltpu.HBM)
    stations = station_cells.shape[0]
    ends = N_SPACE - 1
    upward = [(i, i + 1) for i in range(ends)]
    downward = [(i + 1, i) for i in range(ends)]

    to_left, to_right = pl.pallas_call(
        send_kernel,
        out_shape=(shape(SLAB_PLANE + 1, DEPTH, WIDTH), shape(8, DEPTH, WIDTH)),
        in_specs=[hbm()] * 2,
        out_specs=(vmem(), vmem()),
        scratch_shapes=[
            pltpu.VMEM((2, 2, 3, DEPTH, WIDTH), F32),
            pltpu.VMEM((2, 2, 2, DEPTH, WIDTH), F32),
            pltpu.VMEM((2, 2, 3, DEPTH, WIDTH), F32),
            pltpu.VMEM((1, DEPTH, SLAB), F32),
            pltpu.SemaphoreType.DMA((4,)),
        ],
        compiler_params=params(),
        name="edge_planes",
    )(b_far, pltpu.with_memory_space_constraint(conductivity, pltpu.HBM))
    high = lax.ppermute(to_left, "space", downward)
    low = lax.ppermute(to_right, "space", upward)
    packed = pl.pallas_call(
        pack_kernel,
        out_shape=pltpu.HBM((N_FREQ, 2, DEPTH, 128), F32),
        in_specs=[vmem(), vmem()],
        out_specs=hbm(),
        scratch_shapes=[pltpu.VMEM((2, DEPTH, 128), F32), pltpu.SemaphoreType.DMA((N_FREQ,))],
        compiler_params=params(),
        name="pack_conductivity",
    )(conductivity, high)
    got = lax.all_to_all(packed, "freq", 0, 0, axis_index_groups=[FREQ_ORDER])

    held, u, faces, products, acc = pl.pallas_call(
        curl_kernel,
        out_shape=(
            shape(2, 2, 3, PLANES, DEPTH, WIDTH),
            shape(2, 2, 3, PLANES, DEPTH, WIDTH),
            shape(2, 2, 3, PLANES, DEPTH, WIDTH),
            shape(2, 3, PLANES, DEPTH, WIDTH),
            shape(1, 128),
        ),
        in_specs=[hbm()] + [vmem()] * 2,
        out_specs=(vmem(),) * 5,
        scratch_shapes=[pltpu.VMEM((8, 8, 128), F32), pltpu.SemaphoreType.DMA],
        compiler_params=params(),
        cost_estimate=cost(3.0),
        name="curl_curl",
    )(b_far, low, high)
    sigma, sums = pl.pallas_call(
        moment_kernel,
        out_shape=(shape(PLANES, DEPTH, WIDTH), shape(N_SPACE, 1, 128)),
        in_specs=[smem()] + [vmem()] * 6,
        out_specs=(vmem(),) * 2,
        scratch_shapes=[pltpu.VMEM((DEPTH, WIDTH), F32), pltpu.VMEM((2, 6, 8, 128), F32)],
        compiler_params=params(),
        cost_estimate=cost(2.0),
        name="moments",
    )(frequency, got, held, high, u, faces, acc)
    all_sums = lax.all_to_all(sums, "space", 0, 0, axis_index_groups=[SPACE_ORDER])
    terms = pl.pallas_call(
        sense_kernel,
        out_shape=shape(N_FREQ, DEPTH, 128),
        in_specs=[smem()] + [vmem()] * 3,
        out_specs=vmem(),
        compiler_params=params(),
        cost_estimate=cost(1.0),
        name="sensitivity",
    )(frequency, all_sums, products, sigma)
    shared = lax.all_to_all(terms, "freq", 0, 0, axis_index_groups=[FREQ_ORDER])
    x, sampled = pl.pallas_call(
        field_kernel,
        out_shape=(shape(2, 2, 3, PLANES, DEPTH, WIDTH), shape(2, 2, 3, stations)),
        in_specs=[smem()] + [vmem()] * 6,
        out_specs=(vmem(),) * 2,
        compiler_params=params(),
        cost_estimate=cost(3.0),
        name="field",
    )(frequency, all_sums, held, u, sigma, station_cells[None], station_depth[None])
    gradient = pl.pallas_call(
        gradient_kernel,
        out_shape=shape(PLANES, DEPTH, SLAB),
        in_specs=[vmem()] * 2,
        out_specs=vmem(),
        compiler_params=params(),
        name="gradient",
    )(shared, conductivity)
    return x[None], sampled[None], gradient


def solution(mesh):
    return jax.shard_map(
        local,
        mesh=mesh,
        in_specs=(
            P("freq", None, None, None, "space", None, None),
            P("space", None, "freq"),
            P("freq"),
            P("space"),
            P("space"),
        ),
        out_specs=(
            P("freq", None, None, None, "space", None, None),
            P("freq", None, None, None, "space"),
            P("space", None, "freq"),
        ),
        check_vma=False,
    )
```
